256 devices in a mesh: tm: 16 (over z, y_lo), space: 16 (over y_hi, x, core).
Axes of the slice: x: 4, y: 4 (y_hi: 2, y_lo: 2; y = y_hi * 2 + y_lo), z: 8, core: 2. Of those that a mesh axis runs over, the one named last changes fastest.
Arguments:
- initial: float32 [64, 128, 128], P('space'), may hold values from -6 to 8
- guess: float32 [32, 64, 128, 128], P('tm', 'space'), may hold values from -6 to 8
- conductivity: float32 [64, 128, 128], P('space'), may hold values from 0.1 to 1
- source: float32 [64, 128, 128], P('space'), may hold values from -1.2 to 1.2
Outputs:
- updated: float32 [32, 64, 128, 128], P('tm', 'space')
The draws below stay inside these ranges and needn't reach their ends.
All inputs are finite; a program needn't handle non-finite values.
Results may differ from the reference program's by a relative error of at most 0.00002.
Values sent between devices are 32-bit elements; how exact they have to be, the bound alone decides.
No kernel may reach another device: no remote copies, remote signals or barrier semaphores. Data moves between devices by JAX's collectives and lax.ppermute only.
A program may use at most 64 MiB of HBM per device.

```python
import math
import jax
import jax.numpy as jnp
from jax import lax

NY = 128
NZ = 128
NX = 64
NC = 32


def state_field(key):
    key_pair = jax.random.split(key, 2)
    jitter = jnp.clip(jax.random.normal(key_pair[1], (NX, NY, NZ), jnp.float32), -6.0, 6.0)
    return jitter


def draw_initial(key, part):
    return state_field(key)


def draw_guess(key, part):
    key = jax.random.fold_in(key, 12)
    key_pair = jax.random.split(key, 2)
    jitter = jnp.clip(jax.random.normal(key_pair[1], (NC, NX, NY, NZ), jnp.float32), -6.0, 6.0)
    return jitter


def draw_conductivity(key, part):
    key = jax.random.fold_in(key, 13)
    unit = jax.random.uniform(key, (NX, NY, NZ), jnp.float32, 0.0, 1.0)
    return 0.1 * jnp.exp(unit * math.log(10.0))


def draw_source(key, part):
    key = jax.random.fold_in(key, 14)
    key_pair = jax.random.split(key, 2)
    jitter = jnp.clip(jax.random.normal(key_pair[1], (NX, NY, NZ), jnp.float32), -6.0, 6.0)
    return 0.2 * jitter


def setup_inputs(seed: int = 0) -> dict:
    streams_of = jax.random.split(jax.random.key(seed), 5)
    initial = draw_initial(jax.random.fold_in(streams_of[4], 71), 0)
    guess = draw_guess(jax.random.fold_in(streams_of[4], 71), 0)
    conductivity = draw_conductivity(jax.random.fold_in(streams_of[4], 71), 0)
    source = draw_source(jax.random.fold_in(streams_of[4], 71), 0)
    return dict(initial=initial, guess=guess, conductivity=conductivity, source=source)


fine_rate = 0.04
coarse_rate = 0.16


def divergence(padded_state, padded_cond):
    lead = padded_state.ndim - 3
    state = jnp.pad(padded_state, [(0, 0)] * lead + [(0, 0), (1, 1), (1, 1)])
    cond = jnp.pad(padded_cond, [(0, 0), (1, 1), (1, 1)])
    centre = state[..., 1:-1, 1:-1, 1:-1]
    cond_centre = cond[1:-1, 1:-1, 1:-1]
    pairs = [
        (state[..., 2:, 1:-1, 1:-1], cond[2:, 1:-1, 1:-1]),
        (state[..., :-2, 1:-1, 1:-1], cond[:-2, 1:-1, 1:-1]),
        (state[..., 1:-1, 2:, 1:-1], cond[1:-1, 2:, 1:-1]),
        (state[..., 1:-1, :-2, 1:-1], cond[1:-1, :-2, 1:-1]),
        (state[..., 1:-1, 1:-1, 2:], cond[1:-1, 1:-1, 2:]),
        (state[..., 1:-1, 1:-1, :-2], cond[1:-1, 1:-1, :-2]),
    ]
    total = jnp.zeros(centre.shape, jnp.float32)
    for neighbour, cond_next in pairs:
        total = total + 0.5 * (cond_centre + cond_next) * (neighbour - centre)
    return total


def pad_first(state, cond):
    lead = state.ndim - 3
    padded_state = jnp.pad(state, [(0, 0)] * lead + [(1, 1), (0, 0), (0, 0)])
    padded_cond = jnp.pad(cond, [(1, 1), (0, 0), (0, 0)])
    return padded_state, padded_cond


def fine_step(state, cond, source):
    padded_state, padded_cond = pad_first(state, cond)
    return state + fine_rate * divergence(padded_state, padded_cond) + source


def reference(initial, guess, conductivity, source):
    starts = jnp.concatenate([initial[None], guess[:-1]], 0)
    for turn in range(3):
        starts = fine_step(starts, conductivity, source)
    cvals = fine_step(starts, conductivity, source)
    starts = jnp.concatenate([initial[None], cvals[:-1]], 0)
    for turn in range(3):
        starts = fine_step(starts, conductivity, source)
    resid = fine_step(starts, conductivity, source) - cvals

    def coarse(carry, resid_now):
        padded_state, padded_cond = pad_first(carry, conductivity)
        nxt = carry + coarse_rate * divergence(padded_state, padded_cond) + resid_now
        return nxt, nxt

    _, corr = lax.scan(coarse, jnp.zeros(initial.shape, jnp.float32), resid)
    return cvals + corr
```

```python
import jax
import jax.numpy as jnp
from jax import lax
from jax.experimental import pallas as pl
from jax.experimental.pallas import tpu as pltpu
from jax.sharding import PartitionSpec as P

FINE = 0.04
COARSE = 0.16
NT = 16
NS = 16
PAD = 5
EXT = 4 + 2 * PAD
EVEN = [(i, i ^ 1) for i in range(NS)]
ODD = [(i, (i + 1) % NS if i % 2 else (i - 1) % NS) for i in range(NS)]
VMEM = pl.BlockSpec(memory_space=pltpu.VMEM)
SMEM = pl.BlockSpec(memory_space=pltpu.SMEM)


def place_of(t):
    return t ^ ((t >> 1) & 1)


def y_pairs():
    at = {place_of(t): t for t in range(NT)}
    pairs = []
    for t in range(NT):
        for s in range(NS):
            step = 1 if s % 2 else -1
            pairs.append((t * NS + s, at[(place_of(t) + step) % NT] * NS + (s ^ 1)))
    return pairs


YODD = y_pairs()


def even(x):
    return lax.ppermute(x, "space", EVEN)


def odd(x):
    return lax.ppermute(x, "space", ODD)


def yodd(x):
    return lax.ppermute(x, ("tm", "space"), YODD)


def struct(*shape):
    return jax.ShapeDtypeStruct(shape, jnp.float32)


def params(mib=48):
    return pltpu.CompilerParams(vmem_limit_bytes=mib * 1024 * 1024)


def set_coefficients(cond, kx, ky, kz, bb, lo, hi):
    row = lax.broadcasted_iota(jnp.int32, (128, 128), 0)
    col = lax.broadcasted_iota(jnp.int32, (128, 128), 1)
    inner_row = row < 127
    inner_col = col < 127
    ghosts = (
        (row == 0).astype(jnp.float32)
        + (row == 127).astype(jnp.float32)
        + (col == 0).astype(jnp.float32)
        + (col == 127).astype(jnp.float32)
    ) * (0.5 * FINE)

    @pl.loop(lo, hi)
    def _(l):
        here = cond[l]
        kx[l] = (0.5 * FINE) * (here + cond[l + 1])
        ky[l] = jnp.where(inner_row, (0.5 * FINE) * (here + pltpu.roll(here, 127, 0)), 0.0)
        kz[l] = jnp.where(inner_col, (0.5 * FINE) * (here + pltpu.roll(here, 127, 1)), 0.0)
        bb[l] = ghosts * here


def sweep(read, write, kx, ky, kz, bb, lo, hi):
    start = kx[lo - 1] * (read(lo) - read(lo - 1))

    def layer(l, behind):
        v = read(l)
        ahead = kx[l] * (read(l + 1) - v)
        fy = ky[l] * (pltpu.roll(v, 127, 0) - v)
        fz = kz[l] * (pltpu.roll(v, 127, 1) - v)
        change = (ahead - behind) + (fy - pltpu.roll(fy, 1, 0)) + (fz - pltpu.roll(fz, 1, 1)) - bb[l] * v
        write(l, v, change)
        return ahead

    lax.fori_loop(lo, hi, layer, start)


def clear_outside(s, store):
    @pl.when(s == 0)
    def _():
        for l in range(PAD):
            store(l)

    @pl.when(s == NS - 1)
    def _():
        for l in range(PAD + 4, EXT):
            store(l)


def fine_steps(states, count, widths, cond_refs, heat, s):
    kx, ky, kz, bb = cond_refs
    for turn in range(count):
        a, b = turn % 2, (turn + 1) % 2
        for f in range(2):
            h = widths[f] - 1 - turn

            def write(l, v, change):
                states[b, f, l] = v + change + heat[l]

            sweep(lambda l: states[a, f, l], write, kx, ky, kz, bb, PAD - h, PAD + 4 + h)

        def store(l):
            for f in range(2):
                states[b, f, l] = jnp.zeros((128, 128), jnp.float32)

        clear_outside(s, store)


def first_kernel(flags, g, cond, source, ev, od, out, state, cnd, heat, kx, ky, kz, bb):
    s = flags[1]
    core = s % 2
    for l in range(4):
        for f in range(2):
            state[0, f, PAD + l] = g[f, l]
        cnd[PAD + l] = cond[l]
        heat[PAD + l] = source[l]

    def sides(left, right):
        for l in range(4):
            for f in range(2):
                state[0, f, 1 + l] = left[f, l]
                state[0, f, PAD + 4 + l] = right[f, l]
            cnd[1 + l] = left[2, l]
            cnd[PAD + 4 + l] = right[2, l]
            heat[1 + l] = left[3, l]
            heat[PAD + 4 + l] = right[3, l]

    @pl.when(core == 0)
    def _():
        sides(od, ev)

    @pl.when(core == 1)
    def _():
        sides(ev, od)

    def store(l):
        zero = jnp.zeros((128, 128), jnp.float32)
        for f in range(2):
            state[0, f, l] = zero
        cnd[l] = zero

    clear_outside(s, store)
    set_coefficients(cnd, kx, ky, kz, bb, 1, EXT - 2)
    fine_steps(state, 4, (4, 4), (kx, ky, kz, bb), heat, s)
    for f in range(2):
        for l in range(4):
            out[f, l] = state[0, f, PAD + l]


def second_kernel(flags, a, cond, source, ev, od, evc, odc, ev5, od5, e_out, w_out, state, cnd, heat, kx, ky, kz, bb, wide):
    t, s = flags[0], flags[1]
    core = s % 2
    for l in range(4):
        for f in range(2):
            state[0, f, PAD + l] = a[f, l]
        cnd[PAD + l] = cond[l]
        heat[PAD + l] = source[l]

    def sides(left, right, leftc, rightc, left5, right5):
        for l in range(4):
            for f in range(2):
                state[0, f, 1 + l] = left[f, l]
                state[0, f, PAD + 4 + l] = right[f, l]
            cnd[1 + l] = leftc[2, l]
            cnd[PAD + 4 + l] = rightc[2, l]
            heat[1 + l] = leftc[3, l]
            heat[PAD + 4 + l] = rightc[3, l]
        state[0, 0, 0] = left5[0]
        state[0, 0, EXT - 1] = right5[0]
        cnd[0] = left5[1]
        cnd[EXT - 1] = right5[1]

    @pl.when(core == 0)
    def _():
        sides(od, ev, odc, evc, od5, ev5)

    @pl.when(core == 1)
    def _():
        sides(ev, od, evc, odc, ev5, od5)

    def store(l):
        zero = jnp.zeros((128, 128), jnp.float32)
        for f in range(2):
            state[0, f, l] = zero
        cnd[l] = zero

    clear_outside(s, store)
    set_coefficients(cnd, kx, ky, kz, bb, 0, EXT - 1)
    for f, h in ((0, 1), (1, 0)):

        def keep(l, v, change):
            wide[f, l] = v + (COARSE / FINE) * change

        sweep(lambda l: state[0, f, l], keep, kx, ky, kz, bb, PAD - h, PAD + 4 + h)
    fine_steps(state, 4, (5, 4), (kx, ky, kz, bb), heat, s)
    for l in range(PAD - 1, PAD + 5):
        wide[0, l] = state[0, 0, l] - wide[0, l]
    for l in range(PAD, PAD + 4):
        wide[1, l] = state[0, 1, l] - wide[1, l]

    def clear(l):
        wide[0, l] = jnp.zeros((128, 128), jnp.float32)

    clear_outside(s, clear)
    for l in range(4):
        w_out[l] = wide[0, PAD + l]

    def put(l, value):
        for to in range(NT):
            e_out[to, l] = value[8 * place_of(to) : 8 * place_of(to) + 8]

    def finish(l, v, change):
        wide[1, l] = v + (COARSE / FINE) * change + wide[1, l]

    sweep(lambda l: wide[0, l], finish, kx, ky, kz, bb, PAD, PAD + 4)

    @pl.when(t != NT - 1)
    def _():
        for l in range(4):
            put(l, wide[1, PAD + l])

    @pl.when(t == NT - 1)
    def _():
        for l in range(4):
            put(l, state[0, 0, PAD + l])
            w_out[l] = a[0, l]


def region(flags, cond, halo):
    chip, place = flags[1] // 2, flags[2]
    count = 8 + 2 * halo
    shape = (count, 24, 128)
    layer = lax.broadcasted_iota(jnp.int32, shape, 0) + (chip * 8 - halo)
    row = lax.broadcasted_iota(jnp.int32, shape, 1) + (place * 8 - 8)
    col = lax.broadcasted_iota(jnp.int32, shape, 2)
    inside = (layer >= 0) & (layer < 64) & (row >= 0) & (row < 128)
    mask = inside.astype(jnp.float32)
    c = cond[8 - halo : 16 + halo] * mask
    half = 0.5 * COARSE
    kx = half * (c[:-1] + c[1:])
    ky = half * (c + pltpu.roll(c, 23, 1))
    kz = jnp.where(col < 127, half * (c + pltpu.roll(c, 127, 2)), 0.0)
    bb = jnp.where((col == 0) | (col == 127), half * c, 0.0)
    return mask, kx, ky, kz, bb


def coarse_step(v, coefficients, halo, now):
    mask, kx, ky, kz, bb = coefficients
    skip = halo - now
    count = 8 + 2 * now
    inner = slice(skip + 1, skip + count - 1)
    fx = kx[skip : skip + count - 1] * (v[1:] - v[:-1])
    mid = v[1:-1]
    fy = ky[inner] * (pltpu.roll(mid, 23, 1) - mid)
    fz = kz[inner] * (pltpu.roll(mid, 127, 2) - mid)
    change = (fx[1:] - fx[:-1]) + (fy - pltpu.roll(fy, 1, 1)) + (fz - pltpu.roll(fz, 1, 2)) - bb[inner] * mid
    return mask[inner] * (mid + change)


def store_coefficients(coefficients, refs):
    for value, ref in zip(coefficients, refs):
        ref[...] = value


def gathered(core, own, x_got, x_swap, y_got, y_swap, buf, halo):
    rows = pl.ds(8, 8)
    buf[halo : halo + 8, 8:16] = own

    def put(left, right, below, above):
        buf[:halo, 8:16] = left
        buf[halo + 8 :, 8:16] = right
        buf[:, 0:8] = below
        buf[:, 16:24] = above

    @pl.when(core == 0)
    def _():
        put(x_got(), x_swap(), y_got(), y_swap())

    @pl.when(core == 1)
    def _():
        put(x_swap(), x_got(), y_swap(), y_got())


def pairs_kernel(flags, cond, own, other, xg, xs, yg, ys, p_out, ap_out, send, buf, *coef):
    core = flags[1] % 2
    store_coefficients(region(flags, cond, 2), coef)

    def tile(j):
        k = (j - 1) % NT
        mine, yours = own[k], other[k]
        first = jnp.where(core == 0, mine, yours)
        last = jnp.where(core == 0, yours, mine)
        return jnp.concatenate([first, last], 0)

    for i in range(8):
        gathered(core, tile(2 * i), lambda: xg[i], lambda: xs[i], lambda: yg[i], lambda: ys[i], buf, 2)
        c = tuple(r[...] for r in coef)
        one = coarse_step(buf[...] * c[0], c, 2, 2)
        two = coarse_step(one, c, 2, 1)
        ap_out[i] = one[1:9, 8:16]
        p_out[2 * i] = tile(2 * i)
        p_out[2 * i + 1] = tile(2 * i + 1) + two[:, 8:16]
    for q in range(4):

        @pl.when(core == 0)
        def _():
            send[q] = p_out[4 * q + 1, 0:4]

        @pl.when(core == 1)
        def _():
            send[q] = p_out[4 * q + 1, 4:8]


def half(core, value):
    return jnp.where(core == 0, value[0:4], value[4:8])


def quads_kernel(flags, cond, p, ap, xg, xs, yg, ys, p_out, zp_out, last, done, buf, *coef):
    core = flags[1] % 2
    store_coefficients(region(flags, cond, 4), coef)
    zero = jnp.zeros((4, 8, 128), jnp.float32)
    for q in range(4):
        j = 4 * q
        gathered(core, p[j + 1], lambda: xg[q], lambda: xs[q], lambda: yg[q], lambda: ys[q], buf, 4)
        c = tuple(r[...] for r in coef)
        v = buf[...] * c[0]
        powers = []
        for turn in range(4):
            v = coarse_step(v, c, 4, 4 - turn)
            powers.append(v[3 - turn : 11 - turn, 8:16])
        second = p[j + 2] + powers[1]
        third = p[j + 3] + powers[3]
        partial = [zero, half(core, ap[2 * q]), half(core, powers[0]), half(core, ap[2 * q + 1] + powers[2])]
        ends = [p[j], p[j + 1], second, third]
        if q == 0:
            last[...] = third
            for i in range(4):
                done[i, 0] = partial[i]
                done[i, 1] = half(core, ends[i])
        else:
            for i in range(4):
                p_out[4 * q - 4 + i] = ends[i]
                zp_out[4 * q - 4 + i] = partial[i]


def chain_kernel(q, flags, cond, c_in, p, zp, xg, xs, yg, ys, last, done, buf, *coef):
    core = flags[1] % 2
    store_coefficients(region(flags, cond, 8), coef)
    gathered(core, c_in[...], lambda: xg[...], lambda: xs[...], lambda: yg[...], lambda: ys[...], buf, 8)
    c = tuple(r[...] for r in coef)
    v = buf[...] * c[0]
    for turn in range(8):
        v = coarse_step(v, c, 8, 8 - turn)
        tile = v[7 - turn : 15 - turn, 8:16]
        i = turn // 2
        if turn % 2 == 0:
            done[i, 0] = zp[4 * q - 4 + i] + half(core, tile)
        else:
            full = p[4 * q - 4 + i] + tile
            done[i, 1] = half(core, full)
            if i == 3:
                last[...] = full


def final_kernel(got, w, out):
    for src in range(NT):
        rows = slice(8 * place_of(src), 8 * place_of(src) + 8)
        for l in range(4):
            out[0, l, rows] = got[src, 0, l] + w[l, rows]
            out[1, l, rows] = got[src, 1, l]


def scratch(halo):
    count = 8 + 2 * halo
    return [pltpu.VMEM((count, 24, 128), jnp.float32)] * 2 + [
        pltpu.VMEM((count - 1, 24, 128), jnp.float32),
    ] + [pltpu.VMEM((count, 24, 128), jnp.float32)] * 3


def call(kernel, outs, scratches, *args, smem=True):
    specs = [SMEM] + [VMEM] * (len(args) - 1) if smem else [VMEM] * len(args)
    return pl.pallas_call(
        kernel,
        out_shape=outs,
        in_specs=specs,
        out_specs=[VMEM] * len(outs),
        scratch_shapes=scratches,
        compiler_params=params(),
    )(*args)


def across(own_tile, send, core):
    got = odd(send)
    swap = even(got)
    left = jnp.where(core == 0, got, swap)
    right = jnp.where(core == 0, swap, got)
    wide = jnp.concatenate([left, own_tile, right], 1)
    y_got = yodd(wide)
    y_swap = even(y_got)
    return got, swap, y_got, y_swap


def body(initial, guess, cond, source):
    t = lax.axis_index("tm")
    s = lax.axis_index("space")
    core = s % 2
    place = t ^ ((t >> 1) & 1)
    flags = jnp.stack([t, s, place, core]).astype(jnp.int32)
    g = jnp.stack([jnp.where(t == NT - 1, initial, guess[0]), guess[1]])
    pack = jnp.concatenate([g, cond[None], source[None]])
    ev = even(pack)
    od = odd(pack)
    fine_scratch = [
        pltpu.VMEM((2, 2, EXT, 128, 128), jnp.float32),
    ] + [pltpu.VMEM((EXT, 128, 128), jnp.float32)] * 6
    (a,) = call(first_kernel, [struct(2, 4, 128, 128)], fine_scratch, flags, g, cond, source, ev, od)

    start = 8 * place
    rows_of = lambda x: lax.dynamic_slice_in_dim(jnp.pad(x, ((0, 0), (8, 8), (0, 0))), start, 24, 1)
    mine, yours = rows_of(cond), rows_of(ev[2])
    chip = jnp.where(core == 0, jnp.concatenate([mine, yours]), jnp.concatenate([yours, mine]))
    c_got = odd(chip)
    c_swap = even(c_got)
    tiles = jnp.where(
        core == 0, jnp.concatenate([c_got, chip, c_swap]), jnp.concatenate([c_swap, chip, c_got])
    )

    ev2 = even(a)
    near = lambda x: jnp.where(core == 0, x[0], x[3])
    tail = lambda x: jnp.where(core == 0, x[0], x[3])
    beyond = jnp.stack([tail(ev2[0]), tail(ev[2])])
    od2 = odd(jnp.concatenate([a.reshape(8, 128, 128), beyond]))
    nearest = lambda x: jnp.where(core == 0, x[3], x[0])
    ev5 = even(jnp.stack([nearest(od2[0:4]), nearest(od[2])]))
    e, w = call(
        second_kernel,
        [struct(NT, 4, 8, 128), struct(4, 128, 128)],
        fine_scratch + [pltpu.VMEM((2, EXT, 128, 128), jnp.float32)],
        flags, a, cond, source, ev2, od2[:8].reshape(2, 4, 128, 128), ev, od, ev5, od2[8:],
    )
    w_before = lax.ppermute(w, "tm", [(i, (i + 1) % NT) for i in range(NT)])
    own = lax.all_to_all(e, "tm", 0, 0)
    other = even(own)

    picks = [(2 * i - 1) % NT for i in range(8)]
    mine = jnp.stack([own[k] for k in picks])
    yours = jnp.stack([other[k] for k in picks])
    send = jnp.where(core == 0, mine[:, 0:2], mine[:, 2:4])
    both = jnp.where(core == 0, jnp.concatenate([mine, yours], 1), jnp.concatenate([yours, mine], 1))
    xg, xs, yg, ys = across(both, send, core)
    p, ap, send = call(
        pairs_kernel,
        [struct(NT, 8, 8, 128), struct(8, 8, 8, 128), struct(4, 4, 8, 128)],
        scratch(2),
        flags, tiles, own, other, xg, xs, yg, ys,
    )
    xg, xs, yg, ys = across(jnp.stack([p[1], p[5], p[9], p[13]]), send, core)
    p, zp, last, done = call(
        quads_kernel,
        [struct(12, 8, 8, 128), struct(12, 4, 8, 128), struct(8, 8, 128), struct(4, 2, 4, 8, 128)],
        scratch(4),
        flags, tiles, p, ap, xg, xs, yg, ys,
    )
    parts = [done]
    for q in (1, 2, 3):
        got = across(last[None], last[None], core)
        xg, xs, yg, ys = (x[0] for x in got)
        last, done = call(
            lambda *refs, q=q: chain_kernel(q, *refs),
            [struct(8, 8, 128), struct(4, 2, 4, 8, 128)],
            scratch(8),
            flags, tiles, last, p, zp, xg, xs, yg, ys,
        )
        parts.append(done)
    back = lax.all_to_all(jnp.concatenate(parts), "tm", 0, 0)
    (out,) = call(final_kernel, [struct(2, 4, 128, 128)], [], back, w_before, smem=False)
    return out


def solution(mesh):
    placed = (
        P("space", None, None),
        P("tm", "space", None, None),
        P("space", None, None),
        P("space", None, None),
    )
    return jax.shard_map(
        body, mesh=mesh, in_specs=placed, out_specs=P("tm", "space", None, None), check_vma=False
    )
```

```python
import jax
import jax.numpy as jnp
from jax import lax
from jax.experimental import pallas as pl
from jax.experimental.pallas import tpu as pltpu
from jax.sharding import PartitionSpec as P

FINE = 0.04
COARSE = 0.16
NT = 16
NS = 16
PAD = 5
EXT = 4 + 2 * PAD
EVEN = [(i, i ^ 1) for i in range(NS)]


def odd_pairs():
    pairs = []
    for t in range(NT):
        for s in range(NS):
            to = s + 1 if s % 2 else s - 1
            pairs.append((t * NS + s, t * NS + to if 0 <= to < NS else (t ^ 1) * NS + s))
    return pairs


ODD = odd_pairs()
VMEM = pl.BlockSpec(memory_space=pltpu.VMEM)
SMEM = pl.BlockSpec(memory_space=pltpu.SMEM)


def place_of(t):
    return t ^ ((t >> 1) & 1)


PLACE = [place_of(t) for t in range(NT)]


def y_pairs():
    at = {place_of(t): t for t in range(NT)}
    pairs = []
    for t in range(NT):
        for s in range(NS):
            step = 1 if s % 2 else -1
            pairs.append((t * NS + s, at[(place_of(t) + step) % NT] * NS + (s ^ 1)))
    return pairs


YODD = y_pairs()


def even(x):
    return lax.ppermute(x, "space", EVEN)


def odd(x):
    return lax.ppermute(x, ("tm", "space"), ODD)


def yodd(x):
    return lax.ppermute(x, ("tm", "space"), YODD)


def struct(*shape):
    return jax.ShapeDtypeStruct(shape, jnp.float32)


def params(mib=48):
    return pltpu.CompilerParams(vmem_limit_bytes=mib * 1024 * 1024)


def set_coefficients(cond, kx, ky, kz, aa, lo, hi):
    row = lax.broadcasted_iota(jnp.int32, (128, 128), 0)
    col = lax.broadcasted_iota(jnp.int32, (128, 128), 1)
    ghosts = (
        (row == 0).astype(jnp.float32)
        + (row == 127).astype(jnp.float32)
        + (col == 0).astype(jnp.float32)
        + (col == 127).astype(jnp.float32)
    ) * (0.5 * FINE)
    rows = (row < 127).astype(jnp.float32) * (0.5 * FINE)
    cols = (col < 127).astype(jnp.float32) * (0.5 * FINE)
    for l in range(lo, hi):
        here = cond[l]
        kx[l] = (0.5 * FINE) * (here + cond[l + 1])
        ky[l] = rows * (here + pltpu.roll(here, 127, 0))
        kz[l] = cols * (here + pltpu.roll(here, 127, 1))
        aa[l] = 1.0 - ghosts * here


def rows_at(r):
    return slice(8 * r, 8 * r + 8)


def sweep(read, finish, coefficients, lo, hi):
    kx, ky, kz, aa = coefficients
    sub = lax.broadcasted_iota(jnp.int32, (8, 128), 0)
    bottom, top = sub == 0, sub == 7
    behind = [kx[lo - 1, rows_at(r)] * (read(lo, rows_at(r)) - read(lo - 1, rows_at(r))) for r in range(16)]
    for l in range(lo, hi):
        v = [read(l, rows_at(r)) for r in range(16)]
        rolled = [pltpu.roll(x, 7, 0) for x in v]
        flux = [
            ky[l, rows_at(r)] * ((jnp.where(top, rolled[r + 1], rolled[r]) if r < 15 else rolled[r]) - v[r])
            for r in range(16)
        ]
        back = [pltpu.roll(x, 1, 0) for x in flux]
        ahead = []
        for r in range(16):
            rows = rows_at(r)
            fx = kx[l, rows] * (read(l + 1, rows) - v[r])
            fz = kz[l, rows] * (pltpu.roll(v[r], 127, 1) - v[r])
            down = jnp.where(bottom, back[r - 1] if r else 0.0, back[r])
            total = (aa[l, rows] * v[r] + (fx - behind[r])) + ((flux[r] - down) + (fz - pltpu.roll(fz, 1, 1)))
            finish(l, rows, v[r], total)
            ahead.append(fx)
        behind = ahead


def clear_outside(s, refs, lo, hi):
    zero = jnp.zeros((128, 128), jnp.float32)

    @pl.when(s == 0)
    def _():
        for ref in refs:
            for l in range(lo, PAD):
                ref[l] = zero

    @pl.when(s == NS - 1)
    def _():
        for ref in refs:
            for l in range(PAD + 4, hi):
                ref[l] = zero


def fine_steps(states, widths, coefficients, heat, s):
    for turn in range(4):
        a, b = states[turn % 2], states[1 - turn % 2]
        for f in range(2):
            h = widths[f] - 1 - turn

            def finish(l, rows, v, stepped):
                b[f, l, rows] = stepped + heat[l, rows]

            sweep(lambda l, rows: a[f, l, rows], finish, coefficients, PAD - h, PAD + 4 + h)
        if turn < 3:
            h = max(widths) - 1 - turn
            clear_outside(s, [b.at[0], b.at[1]], PAD - h, PAD + 4 + h)


def first_kernel(flags, g, cond, source, ev, od, out, s0, s1, cnd, heat, *coefficients):
    s = flags[1]
    core = s % 2
    for l in range(4):
        for f in range(2):
            s0[f, PAD + l] = g[f, l]
        cnd[PAD + l] = cond[l]
        heat[PAD + l] = source[l]

    def sides(left, right):
        for l in range(4):
            for f in range(2):
                s0[f, 1 + l] = left[f, l]
                s0[f, PAD + 4 + l] = right[f, l]
            cnd[1 + l] = left[2, l]
            cnd[PAD + 4 + l] = right[2, l]
            heat[1 + l] = left[3, l]
            heat[PAD + 4 + l] = right[3, l]

    @pl.when(core == 0)
    def _():
        sides(od, ev)

    @pl.when(core == 1)
    def _():
        sides(ev, od)

    clear_outside(s, [s0.at[0], s0.at[1], cnd], 1, EXT - 1)
    set_coefficients(cnd, *coefficients, 1, EXT - 2)
    fine_steps((s0, s1), (4, 4), coefficients, heat, s)
    for f in range(2):
        for l in range(4):
            out[f, l] = s0[f, PAD + l]


def second_kernel(
    flags, a, cond, source, ev, od, evc, odc, ev5, chip, e_out, w_out, tiles, s0, s1, cnd, heat, *rest
):
    coefficients, wide = rest[:4], rest[4]
    t, s = flags[0], flags[1]
    core = s % 2
    od_at = lambda i: od[128 * i : 128 * i + 128]
    for l in range(4):
        for f in range(2):
            s0[f, PAD + l] = a[f, l]
        cnd[PAD + l] = cond[l]
        heat[PAD + l] = source[l]
    for l in range(8):
        tiles[8 + l] = chip[l]

    def sides(even, odd, even5, odd5):
        for l in range(4):
            for f in range(2):
                s0[f, even + l] = ev[f, l]
                s0[f, odd + l] = od_at(4 * f + l)
            cnd[even + l] = evc[2, l]
            cnd[odd + l] = odc[2, l]
            heat[even + l] = evc[3, l]
            heat[odd + l] = odc[3, l]
        s0[0, even5] = ev5[0:128]
        s0[0, odd5] = od_at(8)
        cnd[even5] = ev5[128:256]
        cnd[odd5] = od_at(9)

    def side_tiles(even, odd):
        for l in range(8):
            tiles[even + l] = ev5[256 + 24 * l : 280 + 24 * l]
            tiles[odd + l] = od[1280 + 24 * l : 1304 + 24 * l]

    @pl.when(core == 0)
    def _():
        sides(PAD + 4, 1, EXT - 1, 0)
        side_tiles(16, 0)

    @pl.when(core == 1)
    def _():
        sides(1, PAD + 4, 0, EXT - 1)
        side_tiles(0, 16)

    clear_outside(s, [s0.at[0], s0.at[1], cnd], 0, EXT)
    set_coefficients(cnd, *coefficients, 0, EXT - 1)
    ratio = COARSE / FINE
    for f, h in ((0, 1), (1, 0)):

        def keep(l, rows, v, stepped):
            wide[f, l, rows] = v + ratio * (stepped - v)

        sweep(lambda l, rows: s0[f, l, rows], keep, coefficients, PAD - h, PAD + 4 + h)
    fine_steps((s0, s1), (5, 4), coefficients, heat, s)
    for l in range(PAD - 1, PAD + 5):
        wide[0, l] = s0[0, l] - wide[0, l]
    clear_outside(s, [wide.at[0]], PAD - 1, PAD + 5)

    @pl.when(t != NT - 1)
    def _():
        def finish(l, rows, v, stepped):
            to = PLACE[rows.start // 8]
            e_out[to, l - PAD] = v + ratio * (stepped - v) + (s0[1, l, rows] - wide[1, l, rows])

        sweep(lambda l, rows: wide[0, l, rows], finish, coefficients, PAD, PAD + 4)
        for l in range(4):
            w_out[l] = wide[0, PAD + l]

    @pl.when(t == NT - 1)
    def _():
        for l in range(4):
            for r in range(16):
                e_out[PLACE[r], l] = s0[0, PAD + l, rows_at(r)]
            w_out[l] = a[0, l]


def region(flags, cond, halo):
    chip, place = flags[1] // 2, flags[2]
    count = 8 + 2 * halo
    shape = (count, 24, 128)
    layer = lax.broadcasted_iota(jnp.int32, shape, 0) + (chip * 8 - halo)
    row = lax.broadcasted_iota(jnp.int32, shape, 1) + (place * 8 - 8)
    col = lax.broadcasted_iota(jnp.int32, shape, 2)
    inside = (layer >= 0) & (layer < 64) & (row >= 0) & (row < 128)
    mask = inside.astype(jnp.float32)
    c = cond[8 - halo : 16 + halo] * mask
    half = 0.5 * COARSE
    kx = half * (c[:-1] + c[1:])
    ky = half * (c + pltpu.roll(c, 23, 1))
    kz = jnp.where(col < 127, half * (c + pltpu.roll(c, 127, 2)), 0.0)
    bb = jnp.where((col == 0) | (col == 127), half * c, 0.0)
    return mask, kx, ky, kz, bb


def coarse_step(v, coefficients, halo, now):
    mask, kx, ky, kz, bb = coefficients
    skip = halo - now
    count = 8 + 2 * now
    inner = slice(skip + 1, skip + count - 1)
    fx = kx[skip : skip + count - 1] * (v[1:] - v[:-1])
    mid = v[1:-1]
    fy = ky[inner] * (pltpu.roll(mid, 23, 1) - mid)
    fz = kz[inner] * (pltpu.roll(mid, 127, 2) - mid)
    change = (fx[1:] - fx[:-1]) + (fy - pltpu.roll(fy, 1, 1)) + (fz - pltpu.roll(fz, 1, 2)) - bb[inner] * mid
    return mask[inner] * (mid + change)


def store_coefficients(coefficients, refs):
    for value, ref in zip(coefficients, refs):
        ref[...] = value


def gathered(core, own, x_got, x_swap, y_got, y_swap, buf, halo):
    rows = pl.ds(8, 8)
    buf[halo : halo + 8, 8:16] = own

    def put(left, right, below, above):
        buf[:halo, 8:16] = left
        buf[halo + 8 :, 8:16] = right
        buf[:, 0:8] = below
        buf[:, 16:24] = above

    @pl.when(core == 0)
    def _():
        put(x_got(), x_swap(), y_got(), y_swap())

    @pl.when(core == 1)
    def _():
        put(x_swap(), x_got(), y_swap(), y_got())


def pairs_kernel(flags, cond, own, other, xg, xs, yg, ys, p_out, ap_out, send, buf, *coef):
    core = flags[1] % 2
    store_coefficients(region(flags, cond, 2), coef)

    def tile(j):
        k = (j - 1) % NT
        mine, yours = own[k], other[k]
        first = jnp.where(core == 0, mine, yours)
        last = jnp.where(core == 0, yours, mine)
        return jnp.concatenate([first, last], 0)

    for i in range(8):
        gathered(core, tile(2 * i), lambda: xg[i], lambda: xs[i], lambda: yg[i], lambda: ys[i], buf, 2)
        c = tuple(r[...] for r in coef)
        one = coarse_step(buf[...] * c[0], c, 2, 2)
        two = coarse_step(one, c, 2, 1)
        ap_out[i] = one[1:9, 8:16]
        p_out[2 * i] = tile(2 * i)
        p_out[2 * i + 1] = tile(2 * i + 1) + two[:, 8:16]
    for q in range(4):

        @pl.when(core == 0)
        def _():
            send[q] = p_out[4 * q + 1, 0:4]

        @pl.when(core == 1)
        def _():
            send[q] = p_out[4 * q + 1, 4:8]


def half(core, value):
    return jnp.where(core == 0, value[0:4], value[4:8])


def quads_kernel(flags, cond, p, ap, xg, xs, yg, ys, p_out, zp_out, last, done, buf, *coef):
    core = flags[1] % 2
    store_coefficients(region(flags, cond, 4), coef)
    zero = jnp.zeros((4, 8, 128), jnp.float32)
    for q in range(4):
        j = 4 * q
        gathered(core, p[j + 1], lambda: xg[q], lambda: xs[q], lambda: yg[q], lambda: ys[q], buf, 4)
        c = tuple(r[...] for r in coef)
        v = buf[...] * c[0]
        powers = []
        for turn in range(4):
            v = coarse_step(v, c, 4, 4 - turn)
            powers.append(v[3 - turn : 11 - turn, 8:16])
        second = p[j + 2] + powers[1]
        third = p[j + 3] + powers[3]
        partial = [zero, half(core, ap[2 * q]), half(core, powers[0]), half(core, ap[2 * q + 1] + powers[2])]
        ends = [p[j], p[j + 1], second, third]
        if q == 0:
            last[...] = third
            for i in range(4):
                done[i, 0] = partial[i]
                done[i, 1] = half(core, ends[i])
        else:
            for i in range(4):
                p_out[4 * q - 4 + i] = ends[i]
                zp_out[4 * q - 4 + i] = partial[i]


def chain_kernel(q, flags, cond, c_in, p, zp, xg, xs, yg, ys, last, done, buf, *coef):
    core = flags[1] % 2
    store_coefficients(region(flags, cond, 8), coef)
    gathered(core, c_in[...], lambda: xg[...], lambda: xs[...], lambda: yg[...], lambda: ys[...], buf, 8)
    c = tuple(r[...] for r in coef)
    v = buf[...] * c[0]
    for turn in range(8):
        v = coarse_step(v, c, 8, 8 - turn)
        tile = v[7 - turn : 15 - turn, 8:16]
        i = turn // 2
        if turn % 2 == 0:
            done[i, 0] = zp[4 * q - 4 + i] + half(core, tile)
        else:
            full = p[4 * q - 4 + i] + tile
            done[i, 1] = half(core, full)
            if i == 3:
                last[...] = full


def final_kernel(got, w, out):
    for src in range(NT):
        rows = slice(8 * place_of(src), 8 * place_of(src) + 8)
        for l in range(4):
            out[0, l, rows] = got[src, 0, l] + w[l, rows]
            out[1, l, rows] = got[src, 1, l]


def scratch(halo):
    count = 8 + 2 * halo
    return [pltpu.VMEM((count, 24, 128), jnp.float32)] * 2 + [
        pltpu.VMEM((count - 1, 24, 128), jnp.float32),
    ] + [pltpu.VMEM((count, 24, 128), jnp.float32)] * 3


def call(kernel, outs, scratches, *args, smem=True):
    specs = [SMEM] + [VMEM] * (len(args) - 1) if smem else [VMEM] * len(args)
    return pl.pallas_call(
        kernel,
        out_shape=outs,
        in_specs=specs,
        out_specs=[VMEM] * len(outs),
        scratch_shapes=scratches,
        compiler_params=params(),
    )(*args)


def across(own_tile, send, core):
    got = odd(send)
    swap = even(got)
    left = jnp.where(core == 0, got, swap)
    right = jnp.where(core == 0, swap, got)
    wide = jnp.concatenate([left, own_tile, right], 1)
    y_got = yodd(wide)
    y_swap = even(y_got)
    return got, swap, y_got, y_swap


def body(initial, guess, cond, source):
    t = lax.axis_index("tm")
    s = lax.axis_index("space")
    core = s % 2
    place = t ^ ((t >> 1) & 1)
    flags = jnp.stack([t, s, place, core]).astype(jnp.int32)
    g = jnp.stack([jnp.where(t == NT - 1, initial, guess[0]), guess[1]])
    pack = jnp.concatenate([g, cond[None], source[None]])
    ev = even(pack)
    od = odd(pack)
    layers = pltpu.VMEM((EXT, 128, 128), jnp.float32)
    fine_scratch = [pltpu.VMEM((2, EXT, 128, 128), jnp.float32)] * 2 + [layers] * 6
    (a,) = call(first_kernel, [struct(2, 4, 128, 128)], fine_scratch, flags, g, cond, source, ev, od)

    start = 8 * place
    rows_of = lambda x: lax.dynamic_slice_in_dim(jnp.pad(x, ((0, 0), (8, 8), (0, 0))), start, 24, 1)
    mine, yours = rows_of(cond), rows_of(ev[2])
    chip = jnp.where(core == 0, jnp.concatenate([mine, yours]), jnp.concatenate([yours, mine]))

    ev2 = even(a)
    tail = lambda x: jnp.where(core == 0, x[0], x[3])
    nearest = lambda x: jnp.where(core == 0, x[3], x[0])
    chip_rows = chip.reshape(192, 128)
    od2 = odd(jnp.concatenate([a.reshape(1024, 128), tail(ev2[0]), tail(ev[2]), chip_rows]))
    ev5 = even(jnp.concatenate([nearest(od2[:512].reshape(4, 128, 128)), nearest(od[2]), od2[1280:]]))
    e, w, tiles = call(
        second_kernel,
        [struct(NT, 4, 8, 128), struct(4, 128, 128), struct(24, 24, 128)],
        fine_scratch + [pltpu.VMEM((2, EXT, 128, 128), jnp.float32)],
        flags, a, cond, source, ev2, od2, ev, od, ev5, chip,
    )
    w_before = lax.ppermute(w, "tm", [(i, (i + 1) % NT) for i in range(NT)])
    own = lax.all_to_all(e, "tm", 0, 0)
    own, w_before = lax.optimization_barrier((own, w_before))
    other = even(own)

    picks = [(2 * i - 1) % NT for i in range(8)]
    mine = jnp.stack([own[k] for k in picks])
    yours = jnp.stack([other[k] for k in picks])
    send = jnp.where(core == 0, mine[:, 0:2], mine[:, 2:4])
    both = jnp.where(core == 0, jnp.concatenate([mine, yours], 1), jnp.concatenate([yours, mine], 1))
    xg, xs, yg, ys = across(both, send, core)
    p, ap, send = call(
        pairs_kernel,
        [struct(NT, 8, 8, 128), struct(8, 8, 8, 128), struct(4, 4, 8, 128)],
        scratch(2),
        flags, tiles, own, other, xg, xs, yg, ys,
    )
    xg, xs, yg, ys = across(jnp.stack([p[1], p[5], p[9], p[13]]), send, core)
    p, zp, last, done = call(
        quads_kernel,
        [struct(12, 8, 8, 128), struct(12, 4, 8, 128), struct(8, 8, 128), struct(4, 2, 4, 8, 128)],
        scratch(4),
        flags, tiles, p, ap, xg, xs, yg, ys,
    )
    parts = [done]
    for q in (1, 2, 3):
        got = across(last[None], last[None], core)
        xg, xs, yg, ys = (x[0] for x in got)
        last, done = call(
            lambda *refs, q=q: chain_kernel(q, *refs),
            [struct(8, 8, 128), struct(4, 2, 4, 8, 128)],
            scratch(8),
            flags, tiles, last, p, zp, xg, xs, yg, ys,
        )
        parts.append(done)
    back = lax.all_to_all(jnp.concatenate(parts), "tm", 0, 0)
    (out,) = call(final_kernel, [struct(2, 4, 128, 128)], [], back, w_before, smem=False)
    return out


def solution(mesh):
    placed = (
        P("space", None, None),
        P("tm", "space", None, None),
        P("space", None, None),
        P("space", None, None),
    )
    return jax.shard_map(
        body, mesh=mesh, in_specs=placed, out_specs=P("tm", "space", None, None), check_vma=False
    )
```

```python
import functools

import jax
import jax.numpy as jnp
from jax import lax
from jax.experimental import pallas as pl
from jax.experimental.pallas import tpu as pltpu
from jax.sharding import PartitionSpec as P

FINE = 0.04
COARSE = 0.16
NT = 16
NS = 16
PAD = 5
EXT = 4 + 2 * PAD
EVEN = [(i, i ^ 1) for i in range(NS)]


def odd_pairs():
    pairs = []
    for t in range(NT):
        for s in range(NS):
            to = s + 1 if s % 2 else s - 1
            pairs.append((t * NS + s, t * NS + to if 0 <= to < NS else (t ^ 1) * NS + s))
    return pairs


ODD = odd_pairs()
VMEM = pl.BlockSpec(memory_space=pltpu.VMEM)
SMEM = pl.BlockSpec(memory_space=pltpu.SMEM)


def place_of(t):
    return t ^ ((t >> 1) & 1)


PLACE = [place_of(t) for t in range(NT)]


def y_pairs():
    at = {place_of(t): t for t in range(NT)}
    pairs = []
    for t in range(NT):
        for s in range(NS):
            step = 1 if s % 2 else -1
            pairs.append((t * NS + s, at[(place_of(t) + step) % NT] * NS + (s ^ 1)))
    return pairs


YODD = y_pairs()


def even(x):
    return lax.ppermute(x, "space", EVEN)


def odd(x):
    return lax.ppermute(x, ("tm", "space"), ODD)


def yodd(x):
    return lax.ppermute(x, ("tm", "space"), YODD)


def struct(*shape):
    return jax.ShapeDtypeStruct(shape, jnp.float32)


def params(mib=48):
    return pltpu.CompilerParams(vmem_limit_bytes=mib * 1024 * 1024)


def set_coefficients(cond, kx, ky, kz, aa, lo, hi):
    row = lax.broadcasted_iota(jnp.int32, (128, 128), 0)
    col = lax.broadcasted_iota(jnp.int32, (128, 128), 1)
    ghosts = (
        (row == 0).astype(jnp.float32)
        + (row == 127).astype(jnp.float32)
        + (col == 0).astype(jnp.float32)
        + (col == 127).astype(jnp.float32)
    ) * (0.5 * FINE)
    rows = (row < 127).astype(jnp.float32) * (0.5 * FINE)
    cols = (col < 127).astype(jnp.float32) * (0.5 * FINE)
    for l in range(lo, hi):
        here = cond[l]
        kx[l] = (0.5 * FINE) * (here + cond[l + 1])
        ky[l] = rows * (here + pltpu.roll(here, 127, 0))
        kz[l] = cols * (here + pltpu.roll(here, 127, 1))
        aa[l] = 1.0 - ghosts * here


def rows_at(r):
    return slice(8 * r, 8 * r + 8)


def sweep(read, finish, coefficients, lo, hi):
    kx, ky, kz, aa = coefficients
    sub = lax.broadcasted_iota(jnp.int32, (8, 128), 0)
    bottom, top = sub == 0, sub == 7
    behind = [kx[lo - 1, rows_at(r)] * (read(lo, rows_at(r)) - read(lo - 1, rows_at(r))) for r in range(16)]
    for l in range(lo, hi):
        v = [read(l, rows_at(r)) for r in range(16)]
        rolled = [pltpu.roll(x, 7, 0) for x in v]
        flux = [
            ky[l, rows_at(r)] * ((jnp.where(top, rolled[r + 1], rolled[r]) if r < 15 else rolled[r]) - v[r])
            for r in range(16)
        ]
        back = [pltpu.roll(x, 1, 0) for x in flux]
        ahead = []
        for r in range(16):
            rows = rows_at(r)
            fx = kx[l, rows] * (read(l + 1, rows) - v[r])
            fz = kz[l, rows] * (pltpu.roll(v[r], 127, 1) - v[r])
            down = jnp.where(bottom, back[r - 1] if r else 0.0, back[r])
            total = (aa[l, rows] * v[r] + (fx - behind[r])) + ((flux[r] - down) + (fz - pltpu.roll(fz, 1, 1)))
            finish(l, rows, v[r], total)
            ahead.append(fx)
        behind = ahead


def clear_outside(s, refs, lo, hi):
    zero = jnp.zeros((128, 128), jnp.float32)

    @pl.when(s == 0)
    def _():
        for ref in refs:
            for l in range(lo, PAD):
                ref[l] = zero

    @pl.when(s == NS - 1)
    def _():
        for ref in refs:
            for l in range(PAD + 4, hi):
                ref[l] = zero


def fine_steps(states, widths, coefficients, heat, s):
    for turn in range(4):
        a, b = states[turn % 2], states[1 - turn % 2]
        for f in range(2):
            h = widths[f] - 1 - turn

            def finish(l, rows, v, stepped):
                b[f, l, rows] = stepped + heat[l, rows]

            sweep(lambda l, rows: a[f, l, rows], finish, coefficients, PAD - h, PAD + 4 + h)
        if turn < 3:
            h = max(widths) - 1 - turn
            clear_outside(s, [b.at[0], b.at[1]], PAD - h, PAD + 4 + h)


def pack_kernel(flags, initial, guess, cond, source, out):
    @pl.when(flags[0] == NT - 1)
    def _():
        out[0] = initial[...]

    @pl.when(flags[0] != NT - 1)
    def _():
        out[0] = guess[0]

    out[1] = guess[1]
    out[2] = cond[...]
    out[3] = source[...]


def first_kernel(flags, pack, ev, od, out, s0, s1, cnd, heat, *coefficients):
    s = flags[1]
    core = s % 2
    for l in range(4):
        for f in range(2):
            s0[f, PAD + l] = pack[f, l]
        cnd[PAD + l] = pack[2, l]
        heat[PAD + l] = pack[3, l]

    def sides(left, right):
        for l in range(4):
            for f in range(2):
                s0[f, 1 + l] = left[f, l]
                s0[f, PAD + 4 + l] = right[f, l]
            cnd[1 + l] = left[2, l]
            cnd[PAD + 4 + l] = right[2, l]
            heat[1 + l] = left[3, l]
            heat[PAD + 4 + l] = right[3, l]

    @pl.when(core == 0)
    def _():
        sides(od, ev)

    @pl.when(core == 1)
    def _():
        sides(ev, od)

    clear_outside(s, [s0.at[0], s0.at[1], cnd], 1, EXT - 1)
    set_coefficients(cnd, *coefficients, 1, EXT - 2)
    fine_steps((s0, s1), (4, 4), coefficients, heat, s)
    for f in range(2):
        for l in range(4):
            out[f, l] = s0[f, PAD + l]


def second_kernel(
    flags, a, cond, source, ev, od, evc, odc, ev5, chip, e_out, w_out, tiles, s0, s1, cnd, heat, *rest
):
    coefficients, wide = rest[:4], rest[4]
    t, s = flags[0], flags[1]
    core = s % 2
    od_at = lambda i: od[128 * i : 128 * i + 128]
    for l in range(4):
        for f in range(2):
            s0[f, PAD + l] = a[f, l]
        cnd[PAD + l] = cond[l]
        heat[PAD + l] = source[l]
    for l in range(8):
        tiles[8 + l] = chip[l]

    def sides(even, odd, even5, odd5):
        for l in range(4):
            for f in range(2):
                s0[f, even + l] = ev[f, l]
                s0[f, odd + l] = od_at(4 * f + l)
            cnd[even + l] = evc[2, l]
            cnd[odd + l] = odc[2, l]
            heat[even + l] = evc[3, l]
            heat[odd + l] = odc[3, l]
        s0[0, even5] = ev5[0:128]
        s0[0, odd5] = od_at(8)
        cnd[even5] = ev5[128:256]
        cnd[odd5] = od_at(9)

    def side_tiles(even, odd):
        for l in range(8):
            tiles[even + l] = ev5[256 + 24 * l : 280 + 24 * l]
            tiles[odd + l] = od[1280 + 24 * l : 1304 + 24 * l]

    @pl.when(core == 0)
    def _():
        sides(PAD + 4, 1, EXT - 1, 0)
        side_tiles(16, 0)

    @pl.when(core == 1)
    def _():
        sides(1, PAD + 4, 0, EXT - 1)
        side_tiles(0, 16)

    clear_outside(s, [s0.at[0], s0.at[1], cnd], 0, EXT)
    set_coefficients(cnd, *coefficients, 0, EXT - 1)
    ratio = COARSE / FINE
    for f, h in ((0, 1), (1, 0)):

        def keep(l, rows, v, stepped):
            wide[f, l, rows] = v + ratio * (stepped - v)

        sweep(lambda l, rows: s0[f, l, rows], keep, coefficients, PAD - h, PAD + 4 + h)
    fine_steps((s0, s1), (5, 4), coefficients, heat, s)
    for l in range(PAD - 1, PAD + 5):
        wide[0, l] = s0[0, l] - wide[0, l]
    clear_outside(s, [wide.at[0]], PAD - 1, PAD + 5)

    @pl.when(t != NT - 1)
    def _():
        def finish(l, rows, v, stepped):
            to = PLACE[rows.start // 8]
            e_out[to, l - PAD] = v + ratio * (stepped - v) + (s0[1, l, rows] - wide[1, l, rows])

        sweep(lambda l, rows: wide[0, l, rows], finish, coefficients, PAD, PAD + 4)
        for l in range(4):
            w_out[l] = wide[0, PAD + l]

    @pl.when(t == NT - 1)
    def _():
        for l in range(4):
            for r in range(16):
                e_out[PLACE[r], l] = s0[0, PAD + l, rows_at(r)]
            w_out[l] = a[0, l]


def region(flags, cond, halo):
    chip, place = flags[1] // 2, flags[2]
    count = 8 + 2 * halo
    shape = (count, 24, 128)
    layer = lax.broadcasted_iota(jnp.int32, shape, 0) + (chip * 8 - halo)
    row = lax.broadcasted_iota(jnp.int32, shape, 1) + (place * 8 - 8)
    col = lax.broadcasted_iota(jnp.int32, shape, 2)
    inside = (layer >= 0) & (layer < 64) & (row >= 0) & (row < 128)
    mask = inside.astype(jnp.float32)
    c = cond[8 - halo : 16 + halo] * mask
    half = 0.5 * COARSE
    kx = half * (c[:-1] + c[1:])
    ky = half * (c + pltpu.roll(c, 23, 1))
    kz = jnp.where(col < 127, half * (c + pltpu.roll(c, 127, 2)), 0.0)
    bb = jnp.where((col == 0) | (col == 127), half * c, 0.0)
    return mask, kx, ky, kz, bb


def coarse_step(v, coefficients, halo, now):
    mask, kx, ky, kz, bb = coefficients
    skip = halo - now
    count = 8 + 2 * now
    inner = slice(skip + 1, skip + count - 1)
    fx = kx[skip : skip + count - 1] * (v[1:] - v[:-1])
    mid = v[1:-1]
    fy = ky[inner] * (pltpu.roll(mid, 23, 1) - mid)
    fz = kz[inner] * (pltpu.roll(mid, 127, 2) - mid)
    change = (fx[1:] - fx[:-1]) + (fy - pltpu.roll(fy, 1, 1)) + (fz - pltpu.roll(fz, 1, 2)) - bb[inner] * mid
    return mask[inner] * (mid + change)


HALOS = (6, 4, 2)
STARTS = (0, 6, 10, 12)
Y_STARTS = (0, 20, 28, 31)


def half(core, value):
    return jnp.where(core == 0, value[0:4], value[4:8])


def slot(j):
    return (j - 1) % NT


def chips_kernel(flags, own, other, chip, send):
    def run(first, last, side):
        for j in range(NT):
            chip[j, 0:4] = first[slot(j)]
            chip[j, 4:8] = last[slot(j)]
        for q in range(4):
            for i, h in enumerate(HALOS):
                a, b = STARTS[i], STARTS[i] + h
                send[q, a:b] = chip[4 * q + i, side(h)]

    @pl.when(flags[1] % 2 == 0)
    def _():
        run(own, other, lambda h: slice(0, h))

    @pl.when(flags[1] % 2 == 1)
    def _():
        run(other, own, lambda h: slice(8 - h, 8))


def rows_kernel(flags, chip, got, swap, send):
    def run(left, right, upward):
        for q in range(4):
            for i, h in enumerate(HALOS):
                rows = 8 >> i
                pick = slice(8 - rows, 8) if upward else slice(0, rows)
                a = STARTS[i]

                def layer(l):
                    if l < h:
                        return left[q, a + l, pick]
                    if l < h + 8:
                        return chip[4 * q + i, l - h, pick]
                    return right[q, a + l - h - 8, pick]

                per = 8 // rows
                for l in range(8 + 2 * h):
                    k = l % per
                    send[q, Y_STARTS[i] + l // per, rows * k : rows * k + rows] = layer(l)

    @pl.when(flags[1] % 2 == 0)
    def _():
        run(got, swap, False)

    @pl.when(flags[1] % 2 == 1)
    def _():
        run(swap, got, True)


def quads_kernel(flags, cond, chip, xg, xs, yg, ys, p_out, zp_out, ends, last, done, b0, b1, b2, *coef):
    core = flags[1] % 2
    for value, ref in zip(region(flags, cond, 6), coef):
        ref[...] = value
    b1[...] = jnp.zeros((16, 24, 128), jnp.float32)
    b2[...] = jnp.zeros((12, 24, 128), jnp.float32)
    c = tuple(r[...] for r in coef)
    zero = jnp.zeros((4, 8, 128), jnp.float32)
    for q in range(4):

        def fill(left, right, below, above):
            for i, (h, buf) in enumerate(zip(HALOS, (b0, b1, b2))):
                a, rows = STARTS[i], 8 >> i
                buf[h : h + 8, 8:16] = chip[4 * q + i]
                buf[0:h, 8:16] = left[q, a : a + h]
                buf[h + 8 :, 8:16] = right[q, a : a + h]
                per = 8 // rows
                for l in range(8 + 2 * h):
                    k = rows * (l % per)
                    at = Y_STARTS[i] + l // per
                    buf[l, 8 - rows : 8] = below[q, at, k : k + rows]
                    buf[l, 16 : 16 + rows] = above[q, at, k : k + rows]

        @pl.when(core == 0)
        def _():
            fill(xg, xs, yg, ys)

        @pl.when(core == 1)
        def _():
            fill(xs, xg, ys, yg)

        p = b0[...] * c[0]
        values, partial = [chip[4 * q]], [zero]
        for i in range(3):
            h = HALOS[i]
            one = coarse_step(p, c, 6, h)
            two = coarse_step(one, c, 6, h - 1)
            partial.append(half(core, one[h - 1 : h + 7, 8:16]))
            if i < 2:
                p = two + (b1, b2)[i][...] * c[0][2 * i + 2 : 18 - 2 * i]
                values.append(p[h - 2 : h + 6, 8:16])
            else:
                values.append(two[:, 8:16] + chip[4 * q + 3])
        for i in range(4):
            if q == 0:
                done[i, 0] = partial[i]
                done[i, 1] = half(core, values[i])
            else:
                p_out[4 * q - 4 + i] = half(core, values[i])
                zp_out[4 * q - 4 + i] = partial[i]
        if q == 0:
            last[...] = values[3]
        else:
            ends[q - 1] = values[3]


def chain_kernel(q, flags, cond, c_in, p, zp, ends, xg, xs, yg, ys, last, done, buf, *coef):
    core = flags[1] % 2
    for value, ref in zip(region(flags, cond, 8), coef):
        ref[...] = value
    buf[8:16, 8:16] = c_in[...]

    def put(left, right, below, above):
        buf[0:8, 8:16] = left[...]
        buf[16:24, 8:16] = right[...]
        buf[:, 0:8] = below[...]
        buf[:, 16:24] = above[...]

    @pl.when(core == 0)
    def _():
        put(xg, xs, yg, ys)

    @pl.when(core == 1)
    def _():
        put(xs, xg, ys, yg)

    c = tuple(r[...] for r in coef)
    v = buf[...] * c[0]
    for turn in range(8):
        v = coarse_step(v, c, 8, 8 - turn)
        tile = v[7 - turn : 15 - turn, 8:16]
        i = turn // 2
        if turn % 2 == 0:
            done[i, 0] = zp[4 * q - 4 + i] + half(core, tile)
        else:
            done[i, 1] = p[4 * q - 4 + i] + half(core, tile)
    last[...] = ends[q - 1] + tile


def final_kernel(got, w, out):
    for src in range(NT):
        rows = slice(8 * place_of(src), 8 * place_of(src) + 8)
        for l in range(4):
            out[0, l, rows] = got[src, 0, l] + w[l, rows]
            out[1, l, rows] = got[src, 1, l]


def coefficient_scratch(halo):
    counts = [8 + 2 * halo] * 5
    counts[1] -= 1
    return [pltpu.VMEM((count, 24, 128), jnp.float32) for count in counts]


def call(kernel, outs, scratches, *args, smem=True):
    specs = [SMEM] + [VMEM] * (len(args) - 1) if smem else [VMEM] * len(args)
    return pl.pallas_call(
        kernel,
        out_shape=outs,
        in_specs=specs,
        out_specs=[VMEM] * len(outs),
        scratch_shapes=scratches,
        compiler_params=params(),
    )(*args)


def body(initial, guess, cond, source):
    t = lax.axis_index("tm")
    s = lax.axis_index("space")
    core = s % 2
    place = t ^ ((t >> 1) & 1)
    flags = jnp.stack([t, s, place, core]).astype(jnp.int32)
    (pack,) = call(pack_kernel, [struct(4, 4, 128, 128)], [], flags, initial, guess, cond, source)
    ev = even(pack)
    od = odd(pack)
    layers = pltpu.VMEM((EXT, 128, 128), jnp.float32)
    fine_scratch = [pltpu.VMEM((2, EXT, 128, 128), jnp.float32)] * 2 + [layers] * 6
    (a,) = call(first_kernel, [struct(2, 4, 128, 128)], fine_scratch, flags, pack, ev, od)

    start = 8 * place
    rows_of = lambda x: lax.dynamic_slice_in_dim(jnp.pad(x, ((0, 0), (8, 8), (0, 0))), start, 24, 1)
    mine, yours = rows_of(cond), rows_of(ev[2])
    chip = jnp.where(core == 0, jnp.concatenate([mine, yours]), jnp.concatenate([yours, mine]))

    ev2 = even(a)
    tail = lambda x: jnp.where(core == 0, x[0], x[3])
    nearest = lambda x: jnp.where(core == 0, x[3], x[0])
    chip_rows = chip.reshape(192, 128)
    od2 = odd(jnp.concatenate([a.reshape(1024, 128), tail(ev2[0]), tail(ev[2]), chip_rows]))
    ev5 = even(jnp.concatenate([nearest(od2[:512].reshape(4, 128, 128)), nearest(od[2]), od2[1280:]]))
    e, w, tiles = call(
        second_kernel,
        [struct(NT, 4, 8, 128), struct(4, 128, 128), struct(24, 24, 128)],
        fine_scratch + [pltpu.VMEM((2, EXT, 128, 128), jnp.float32)],
        flags, a, cond, source, ev2, od2, ev, od, ev5, chip,
    )
    w_before = lax.ppermute(w, "tm", [(i, (i + 1) % NT) for i in range(NT)])
    own = lax.all_to_all(e, "tm", 0, 0)
    other = even(own)
    chips, send = call(chips_kernel, [struct(NT, 8, 8, 128), struct(4, 12, 8, 128)], [], flags, own, other)
    xg = odd(send)
    xs = even(xg)
    (send,) = call(rows_kernel, [struct(4, 31, 8, 128)], [], flags, chips, xg, xs)
    yg = yodd(send)
    ys = even(yg)
    regions = [pltpu.VMEM((8 + 2 * h, 24, 128), jnp.float32) for h in HALOS]
    p, zp, ends, last, done = call(
        quads_kernel,
        [
            struct(12, 4, 8, 128),
            struct(12, 4, 8, 128),
            struct(3, 8, 8, 128),
            struct(8, 8, 128),
            struct(4, 2, 4, 8, 128),
        ],
        regions + coefficient_scratch(6),
        flags, tiles, chips, xg, xs, yg, ys,
    )
    parts = [done]
    for q in (1, 2, 3):
        xg = odd(last)
        xs = even(xg)
        left = jnp.where(core == 0, xg, xs)
        right = jnp.where(core == 0, xs, xg)
        yg = yodd(jnp.concatenate([left, last, right]))
        ys = even(yg)
        last, done = call(
            functools.partial(chain_kernel, q),
            [struct(8, 8, 128), struct(4, 2, 4, 8, 128)],
            [pltpu.VMEM((24, 24, 128), jnp.float32)] + coefficient_scratch(8),
            flags, tiles, last, p, zp, ends, xg, xs, yg, ys,
        )
        if q == 2:
            last, w_before = lax.optimization_barrier((last, w_before))
        parts.append(done)
    back = lax.all_to_all(jnp.concatenate(parts), "tm", 0, 0)
    (out,) = call(final_kernel, [struct(2, 4, 128, 128)], [], back, w_before, smem=False)
    return out


def solution(mesh):
    placed = (
        P("space", None, None),
        P("tm", "space", None, None),
        P("space", None, None),
        P("space", None, None),
    )
    return jax.shard_map(
        body, mesh=mesh, in_specs=placed, out_specs=P("tm", "space", None, None), check_vma=False
    )
```

```python
import functools

import jax
import jax.numpy as jnp
from jax import lax
from jax.experimental import pallas as pl
from jax.experimental.pallas import tpu as pltpu
from jax.sharding import PartitionSpec as P

FINE = 0.04
COARSE = 0.16
NT = 16
NS = 16
PAD = 5
EXT = 4 + 2 * PAD
EVEN = [(i, i ^ 1) for i in range(NS)]


def odd_pairs():
    pairs = []
    for t in range(NT):
        for s in range(NS):
            to = s + 1 if s % 2 else s - 1
            pairs.append((t * NS + s, t * NS + to if 0 <= to < NS else (t ^ 2) * NS + s))
    return pairs


ODD = odd_pairs()
VMEM = pl.BlockSpec(memory_space=pltpu.VMEM)
SMEM = pl.BlockSpec(memory_space=pltpu.SMEM)


def place_of(t):
    return t ^ ((t >> 1) & 1)


PLACE = [place_of(t) for t in range(NT)]


def y_pairs():
    at = {place_of(t): t for t in range(NT)}
    pairs = []
    for t in range(NT):
        for s in range(NS):
            step = 1 if s % 2 else -1
            pairs.append((t * NS + s, at[(place_of(t) + step) % NT] * NS + (s ^ 1)))
    return pairs


YODD = y_pairs()


def even(x):
    return lax.ppermute(x, "space", EVEN)


def odd(x):
    return lax.ppermute(x, ("tm", "space"), ODD)


def yodd(x):
    return lax.ppermute(x, ("tm", "space"), YODD)


def struct(*shape):
    return jax.ShapeDtypeStruct(shape, jnp.float32)


def params(mib=48):
    return pltpu.CompilerParams(vmem_limit_bytes=mib * 1024 * 1024)


def set_coefficients(cond, kx, ky, kz, aa, lo, hi):
    row = lax.broadcasted_iota(jnp.int32, (128, 128), 0)
    col = lax.broadcasted_iota(jnp.int32, (128, 128), 1)
    ghosts = (
        (row == 0).astype(jnp.float32)
        + (row == 127).astype(jnp.float32)
        + (col == 0).astype(jnp.float32)
        + (col == 127).astype(jnp.float32)
    ) * (0.5 * FINE)
    rows = (row < 127).astype(jnp.float32) * (0.5 * FINE)
    cols = (col < 127).astype(jnp.float32) * (0.5 * FINE)
    for l in range(lo, hi):
        here = cond[l]
        kx[l] = (0.5 * FINE) * (here + cond[l + 1])
        ky[l] = rows * (here + pltpu.roll(here, 127, 0))
        kz[l] = cols * (here + pltpu.roll(here, 127, 1))
        aa[l] = 1.0 - ghosts * here


def rows_at(r):
    return slice(8 * r, 8 * r + 8)


def sweep(read, finish, coefficients, lo, hi):
    kx, ky, kz, aa = coefficients
    sub = lax.broadcasted_iota(jnp.int32, (8, 128), 0)
    bottom, top = sub == 0, sub == 7
    behind = [kx[lo - 1, rows_at(r)] * (read(lo, rows_at(r)) - read(lo - 1, rows_at(r))) for r in range(16)]
    for l in range(lo, hi):
        v = [read(l, rows_at(r)) for r in range(16)]
        rolled = [pltpu.roll(x, 7, 0) for x in v]
        flux = [
            ky[l, rows_at(r)] * ((jnp.where(top, rolled[r + 1], rolled[r]) if r < 15 else rolled[r]) - v[r])
            for r in range(16)
        ]
        back = [pltpu.roll(x, 1, 0) for x in flux]
        ahead = []
        for r in range(16):
            rows = rows_at(r)
            fx = kx[l, rows] * (read(l + 1, rows) - v[r])
            fz = kz[l, rows] * (pltpu.roll(v[r], 127, 1) - v[r])
            down = jnp.where(bottom, back[r - 1] if r else 0.0, back[r])
            total = (aa[l, rows] * v[r] + (fx - behind[r])) + ((flux[r] - down) + (fz - pltpu.roll(fz, 1, 1)))
            finish(l, rows, v[r], total)
            ahead.append(fx)
        behind = ahead


def clear_outside(s, refs, lo, hi):
    zero = jnp.zeros((128, 128), jnp.float32)

    @pl.when(s == 0)
    def _():
        for ref in refs:
            for l in range(lo, PAD):
                ref[l] = zero

    @pl.when(s == NS - 1)
    def _():
        for ref in refs:
            for l in range(PAD + 4, hi):
                ref[l] = zero


def fine_steps(states, widths, coefficients, heat, s):
    for turn in range(4):
        a, b = states[turn % 2], states[1 - turn % 2]
        for f in range(2):
            h = widths[f] - 1 - turn

            def finish(l, rows, v, stepped):
                b[f, l, rows] = stepped + heat[l, rows]

            sweep(lambda l, rows: a[f, l, rows], finish, coefficients, PAD - h, PAD + 4 + h)
        if turn < 3:
            h = max(widths) - 1 - turn
            clear_outside(s, [b.at[0], b.at[1]], PAD - h, PAD + 4 + h)


def first_kernel(flags, pack, ev, od, out, s0, s1, cnd, heat, *coefficients):
    s = flags[1]
    core = s % 2
    for l in range(4):
        for f in range(2):
            s0[f, PAD + l] = pack[f, l]
        cnd[PAD + l] = pack[2, l]
        heat[PAD + l] = pack[3, l]

    def sides(left, right):
        for l in range(4):
            for f in range(2):
                s0[f, 1 + l] = left[f, l]
                s0[f, PAD + 4 + l] = right[f, l]
            cnd[1 + l] = left[2, l]
            cnd[PAD + 4 + l] = right[2, l]
            heat[1 + l] = left[3, l]
            heat[PAD + 4 + l] = right[3, l]

    @pl.when(core == 0)
    def _():
        sides(od, ev)

    @pl.when(core == 1)
    def _():
        sides(ev, od)

    clear_outside(s, [s0.at[0], s0.at[1], cnd], 1, EXT - 1)
    set_coefficients(cnd, *coefficients, 1, EXT - 2)
    fine_steps((s0, s1), (4, 4), coefficients, heat, s)
    for f in range(2):
        for l in range(4):
            out[f, l] = s0[f, PAD + l]


def second_kernel(
    flags, a, pack, ev, od, evc, odc, ev5, chip, e_out, w_out, tiles, s0, s1, cnd, heat, *rest
):
    coefficients, wide = rest[:4], rest[4]
    t, s = flags[0], flags[1]
    core = s % 2
    od_at = lambda i: od[128 * i : 128 * i + 128]
    for l in range(4):
        for f in range(2):
            s0[f, PAD + l] = a[f, l]
        cnd[PAD + l] = pack[2, l]
        heat[PAD + l] = pack[3, l]
    for l in range(8):
        tiles[8 + l] = chip[l]

    def sides(even, odd, even5, odd5):
        for l in range(4):
            for f in range(2):
                s0[f, even + l] = ev[f, l]
                s0[f, odd + l] = od_at(4 * f + l)
            cnd[even + l] = evc[2, l]
            cnd[odd + l] = odc[2, l]
            heat[even + l] = evc[3, l]
            heat[odd + l] = odc[3, l]
        s0[0, even5] = ev5[0:128]
        s0[0, odd5] = od_at(8)
        cnd[even5] = ev5[128:256]
        cnd[odd5] = od_at(9)

    def side_tiles(even, odd):
        for l in range(8):
            tiles[even + l] = ev5[256 + 24 * l : 280 + 24 * l]
            tiles[odd + l] = od[1280 + 24 * l : 1304 + 24 * l]

    @pl.when(core == 0)
    def _():
        sides(PAD + 4, 1, EXT - 1, 0)
        side_tiles(16, 0)

    @pl.when(core == 1)
    def _():
        sides(1, PAD + 4, 0, EXT - 1)
        side_tiles(0, 16)

    clear_outside(s, [s0.at[0], s0.at[1], cnd], 0, EXT)
    set_coefficients(cnd, *coefficients, 0, EXT - 1)
    ratio = COARSE / FINE
    for f, h in ((0, 1), (1, 0)):

        def keep(l, rows, v, stepped):
            wide[f, l, rows] = v + ratio * (stepped - v)

        sweep(lambda l, rows: s0[f, l, rows], keep, coefficients, PAD - h, PAD + 4 + h)
    fine_steps((s0, s1), (5, 4), coefficients, heat, s)
    for l in range(PAD - 1, PAD + 5):
        wide[0, l] = s0[0, l] - wide[0, l]
    clear_outside(s, [wide.at[0]], PAD - 1, PAD + 5)

    @pl.when(t != NT - 1)
    def _():
        def finish(l, rows, v, stepped):
            to = PLACE[rows.start // 8]
            e_out[to, l - PAD] = v + ratio * (stepped - v) + (s0[1, l, rows] - wide[1, l, rows])

        sweep(lambda l, rows: wide[0, l, rows], finish, coefficients, PAD, PAD + 4)
        for l in range(4):
            w_out[l] = wide[0, PAD + l]

    @pl.when(t == NT - 1)
    def _():
        for l in range(4):
            for r in range(16):
                e_out[PLACE[r], l] = s0[0, PAD + l, rows_at(r)]
            w_out[l] = a[0, l]


def region(flags, cond, halo):
    chip, place = flags[1] // 2, flags[2]
    count = 8 + 2 * halo
    shape = (count, 24, 128)
    layer = lax.broadcasted_iota(jnp.int32, shape, 0) + (chip * 8 - halo)
    row = lax.broadcasted_iota(jnp.int32, shape, 1) + (place * 8 - 8)
    col = lax.broadcasted_iota(jnp.int32, shape, 2)
    inside = (layer >= 0) & (layer < 64) & (row >= 0) & (row < 128)
    mask = inside.astype(jnp.float32)
    c = cond[8 - halo : 16 + halo] * mask
    half = 0.5 * COARSE
    kx = half * (c[:-1] + c[1:])
    ky = half * (c + pltpu.roll(c, 23, 1))
    kz = jnp.where(col < 127, half * (c + pltpu.roll(c, 127, 2)), 0.0)
    bb = jnp.where((col == 0) | (col == 127), half * c, 0.0)
    return mask, kx, ky, kz, bb


def coarse_step(v, coefficients, halo, now):
    mask, kx, ky, kz, bb = coefficients
    skip = halo - now
    count = 8 + 2 * now
    inner = slice(skip + 1, skip + count - 1)
    fx = kx[skip : skip + count - 1] * (v[1:] - v[:-1])
    mid = v[1:-1]
    fy = ky[inner] * (pltpu.roll(mid, 23, 1) - mid)
    fz = kz[inner] * (pltpu.roll(mid, 127, 2) - mid)
    change = (fx[1:] - fx[:-1]) + (fy - pltpu.roll(fy, 1, 1)) + (fz - pltpu.roll(fz, 1, 2)) - bb[inner] * mid
    return mask[inner] * (mid + change)


HALOS = (6, 4, 2)
STARTS = (0, 6, 10, 12)
Y_STARTS = (0, 20, 28, 31)


def half(core, value):
    return jnp.where(core == 0, value[0:4], value[4:8])


def slot(j):
    return (j - 1) % NT


def chips_kernel(flags, own, other, chip, send):
    def run(first, last, side):
        for j in range(NT):
            chip[j, 0:4] = first[slot(j)]
            chip[j, 4:8] = last[slot(j)]
        for q in range(4):
            for i, h in enumerate(HALOS):
                a, b = STARTS[i], STARTS[i] + h
                send[q, a:b] = chip[4 * q + i, side(h)]

    @pl.when(flags[1] % 2 == 0)
    def _():
        run(own, other, lambda h: slice(0, h))

    @pl.when(flags[1] % 2 == 1)
    def _():
        run(other, own, lambda h: slice(8 - h, 8))


def rows_kernel(flags, chip, got, swap, send):
    def run(left, right, upward):
        for q in range(4):
            for i, h in enumerate(HALOS):
                rows = 8 >> i
                pick = slice(8 - rows, 8) if upward else slice(0, rows)
                a = STARTS[i]

                def layer(l):
                    if l < h:
                        return left[q, a + l, pick]
                    if l < h + 8:
                        return chip[4 * q + i, l - h, pick]
                    return right[q, a + l - h - 8, pick]

                per = 8 // rows
                for l in range(8 + 2 * h):
                    k = l % per
                    send[q, Y_STARTS[i] + l // per, rows * k : rows * k + rows] = layer(l)

    @pl.when(flags[1] % 2 == 0)
    def _():
        run(got, swap, False)

    @pl.when(flags[1] % 2 == 1)
    def _():
        run(swap, got, True)


def quads_kernel(flags, cond, chip, xg, xs, yg, ys, p_out, zp_out, ends, last, done, b0, b1, b2, *coef):
    core = flags[1] % 2
    for value, ref in zip(region(flags, cond, 6), coef):
        ref[...] = value
    b1[...] = jnp.zeros((16, 24, 128), jnp.float32)
    b2[...] = jnp.zeros((12, 24, 128), jnp.float32)
    c = tuple(r[...] for r in coef)
    zero = jnp.zeros((4, 8, 128), jnp.float32)
    for q in range(4):

        def fill(left, right, below, above):
            for i, (h, buf) in enumerate(zip(HALOS, (b0, b1, b2))):
                a, rows = STARTS[i], 8 >> i
                buf[h : h + 8, 8:16] = chip[4 * q + i]
                buf[0:h, 8:16] = left[q, a : a + h]
                buf[h + 8 :, 8:16] = right[q, a : a + h]
                per = 8 // rows
                for l in range(8 + 2 * h):
                    k = rows * (l % per)
                    at = Y_STARTS[i] + l // per
                    buf[l, 8 - rows : 8] = below[q, at, k : k + rows]
                    buf[l, 16 : 16 + rows] = above[q, at, k : k + rows]

        @pl.when(core == 0)
        def _():
            fill(xg, xs, yg, ys)

        @pl.when(core == 1)
        def _():
            fill(xs, xg, ys, yg)

        p = b0[...] * c[0]
        values, partial = [chip[4 * q]], [zero]
        for i in range(3):
            h = HALOS[i]
            one = coarse_step(p, c, 6, h)
            two = coarse_step(one, c, 6, h - 1)
            partial.append(half(core, one[h - 1 : h + 7, 8:16]))
            if i < 2:
                p = two + (b1, b2)[i][...] * c[0][2 * i + 2 : 18 - 2 * i]
                values.append(p[h - 2 : h + 6, 8:16])
            else:
                values.append(two[:, 8:16] + chip[4 * q + 3])
        for i in range(4):
            if q == 0:
                done[i, 0] = partial[i]
                done[i, 1] = half(core, values[i])
            else:
                p_out[4 * q - 4 + i] = half(core, values[i])
                zp_out[4 * q - 4 + i] = partial[i]
        if q == 0:
            last[...] = values[3]
        else:
            ends[q - 1] = values[3]


def chain_kernel(q, flags, cond, c_in, p, zp, ends, xg, xs, yg, ys, last, done, buf, *coef):
    core = flags[1] % 2
    for value, ref in zip(region(flags, cond, 8), coef):
        ref[...] = value
    buf[8:16, 8:16] = c_in[...]

    def put(left, right, below, above):
        buf[0:8, 8:16] = left[...]
        buf[16:24, 8:16] = right[...]
        buf[:, 0:8] = below[...]
        buf[:, 16:24] = above[...]

    @pl.when(core == 0)
    def _():
        put(xg, xs, yg, ys)

    @pl.when(core == 1)
    def _():
        put(xs, xg, ys, yg)

    c = tuple(r[...] for r in coef)
    v = buf[...] * c[0]
    for turn in range(8):
        v = coarse_step(v, c, 8, 8 - turn)
        tile = v[7 - turn : 15 - turn, 8:16]
        i = turn // 2
        if turn % 2 == 0:
            done[i, 0] = zp[4 * q - 4 + i] + half(core, tile)
        else:
            done[i, 1] = p[4 * q - 4 + i] + half(core, tile)
    last[...] = ends[q - 1] + tile


def final_kernel(got, w, out):
    for src in range(NT):
        rows = slice(8 * place_of(src), 8 * place_of(src) + 8)
        for l in range(4):
            out[0, l, rows] = got[src, 0, l] + w[l, rows]
            out[1, l, rows] = got[src, 1, l]


def coefficient_scratch(halo):
    counts = [8 + 2 * halo] * 5
    counts[1] -= 1
    return [pltpu.VMEM((count, 24, 128), jnp.float32) for count in counts]


def call(kernel, outs, scratches, *args, smem=True):
    specs = [SMEM] + [VMEM] * (len(args) - 1) if smem else [VMEM] * len(args)
    return pl.pallas_call(
        kernel,
        out_shape=outs,
        in_specs=specs,
        out_specs=[VMEM] * len(outs),
        scratch_shapes=scratches,
        compiler_params=params(),
    )(*args)


def body(initial, guess, cond, source):
    t = lax.axis_index("tm")
    s = lax.axis_index("space")
    core = s % 2
    place = t ^ ((t >> 1) & 1)
    flags = jnp.stack([t, s, place, core]).astype(jnp.int32)
    swap = (jnp.arange(4) == 0)[:, None, None, None] & (t == NT - 1)
    pack = jnp.where(swap, initial[None], jnp.concatenate([guess, cond[None], source[None]]))
    ev = even(pack)
    od = odd(pack)
    layers = pltpu.VMEM((EXT, 128, 128), jnp.float32)
    fine_scratch = [pltpu.VMEM((2, EXT, 128, 128), jnp.float32)] * 2 + [layers] * 6
    (a,) = call(first_kernel, [struct(2, 4, 128, 128)], fine_scratch, flags, pack, ev, od)

    start = 8 * place
    rows_of = lambda x: lax.dynamic_slice_in_dim(jnp.pad(x, ((0, 0), (8, 8), (0, 0))), start, 24, 1)
    mine, yours = rows_of(pack[2]), rows_of(ev[2])
    chip = jnp.where(core == 0, jnp.concatenate([mine, yours]), jnp.concatenate([yours, mine]))

    ev2 = even(a)
    tail = lambda x: jnp.where(core == 0, x[0], x[3])
    nearest = lambda x: jnp.where(core == 0, x[3], x[0])
    chip_rows = chip.reshape(192, 128)
    od2 = odd(jnp.concatenate([a.reshape(1024, 128), tail(ev2[0]), tail(ev[2]), chip_rows]))
    ev5 = even(jnp.concatenate([nearest(od2[:512].reshape(4, 128, 128)), nearest(od[2]), od2[1280:]]))
    e, w, tiles = call(
        second_kernel,
        [struct(NT, 4, 8, 128), struct(4, 128, 128), struct(24, 24, 128)],
        fine_scratch + [pltpu.VMEM((2, EXT, 128, 128), jnp.float32)],
        flags, a, pack, ev2, od2, ev, od, ev5, chip,
    )
    own = lax.all_to_all(e, "tm", 0, 0)
    own, w = lax.optimization_barrier((own, w))
    w_before = lax.ppermute(w, "tm", [(i, (i + 1) % NT) for i in range(NT)])
    other = even(own)
    chips, send = call(chips_kernel, [struct(NT, 8, 8, 128), struct(4, 12, 8, 128)], [], flags, own, other)
    xg = odd(send)
    xs = even(xg)
    (send,) = call(rows_kernel, [struct(4, 31, 8, 128)], [], flags, chips, xg, xs)
    send, w_before = lax.optimization_barrier((send, w_before))
    yg = yodd(send)
    ys = even(yg)
    regions = [pltpu.VMEM((8 + 2 * h, 24, 128), jnp.float32) for h in HALOS]
    p, zp, ends, last, done = call(
        quads_kernel,
        [
            struct(12, 4, 8, 128),
            struct(12, 4, 8, 128),
            struct(3, 8, 8, 128),
            struct(8, 8, 128),
            struct(4, 2, 4, 8, 128),
        ],
        regions + coefficient_scratch(6),
        flags, tiles, chips, xg, xs, yg, ys,
    )
    parts = [done]
    for q in (1, 2, 3):
        xg = odd(last)
        xs = even(xg)
        left = jnp.where(core == 0, xg, xs)
        right = jnp.where(core == 0, xs, xg)
        yg = yodd(jnp.concatenate([left, last, right]))
        ys = even(yg)
        last, done = call(
            functools.partial(chain_kernel, q),
            [struct(8, 8, 128), struct(4, 2, 4, 8, 128)],
            [pltpu.VMEM((24, 24, 128), jnp.float32)] + coefficient_scratch(8),
            flags, tiles, last, p, zp, ends, xg, xs, yg, ys,
        )
        parts.append(done)
    back = lax.all_to_all(jnp.concatenate(parts), "tm", 0, 0)
    (out,) = call(final_kernel, [struct(2, 4, 128, 128)], [], back, w_before, smem=False)
    return out


def solution(mesh):
    placed = (
        P("space", None, None),
        P("tm", "space", None, None),
        P("space", None, None),
        P("space", None, None),
    )
    return jax.shard_map(
        body, mesh=mesh, in_specs=placed, out_specs=P("tm", "space", None, None), check_vma=False
    )
```

```python
import functools

import jax
import jax.numpy as jnp
from jax import lax
from jax.experimental import pallas as pl
from jax.experimental.pallas import tpu as pltpu
from jax.sharding import PartitionSpec as P

FINE = 0.04
COARSE = 0.16
NT = 16
NS = 16
PAD = 5
EXT = 4 + 2 * PAD
EVEN = [(i, i ^ 1) for i in range(NS)]


def odd_pairs():
    pairs = []
    for t in range(NT):
        for s in range(NS):
            to = s + 1 if s % 2 else s - 1
            pairs.append((t * NS + s, t * NS + to if 0 <= to < NS else (t ^ 2) * NS + s))
    return pairs


ODD = odd_pairs()
VMEM = pl.BlockSpec(memory_space=pltpu.VMEM)
SMEM = pl.BlockSpec(memory_space=pltpu.SMEM)


def place_of(t):
    return t ^ ((t >> 1) & 1)


PLACE = [place_of(t) for t in range(NT)]


def y_pairs():
    at = {place_of(t): t for t in range(NT)}
    pairs = []
    for t in range(NT):
        for s in range(NS):
            step = 1 if s % 2 else -1
            pairs.append((t * NS + s, at[(place_of(t) + step) % NT] * NS + (s ^ 1)))
    return pairs


YODD = y_pairs()


def even(x):
    return lax.ppermute(x, "space", EVEN)


def odd(x):
    return lax.ppermute(x, ("tm", "space"), ODD)


def yodd(x):
    return lax.ppermute(x, ("tm", "space"), YODD)


def struct(*shape):
    return jax.ShapeDtypeStruct(shape, jnp.float32)


def params(mib=48):
    return pltpu.CompilerParams(vmem_limit_bytes=mib * 1024 * 1024)


def set_coefficients(cond, kx, ky, kz, aa, lo, hi):
    row = lax.broadcasted_iota(jnp.int32, (128, 128), 0)
    col = lax.broadcasted_iota(jnp.int32, (128, 128), 1)
    ghosts = (
        (row == 0).astype(jnp.float32)
        + (row == 127).astype(jnp.float32)
        + (col == 0).astype(jnp.float32)
        + (col == 127).astype(jnp.float32)
    ) * (0.5 * FINE)
    rows = (row < 127).astype(jnp.float32) * (0.5 * FINE)
    cols = (col < 127).astype(jnp.float32) * (0.5 * FINE)
    for l in range(lo, hi):
        here = cond[l]
        kx[l] = (0.5 * FINE) * (here + cond[l + 1])
        ky[l] = rows * (here + pltpu.roll(here, 127, 0))
        kz[l] = cols * (here + pltpu.roll(here, 127, 1))
        aa[l] = 1.0 - ghosts * here


def rows_at(r):
    return slice(8 * r, 8 * r + 8)


def sweep(read, finish, coefficients, lo, hi):
    kx, ky, kz, aa = coefficients
    sub = lax.broadcasted_iota(jnp.int32, (8, 128), 0)
    bottom, top = sub == 0, sub == 7
    behind = [kx[lo - 1, rows_at(r)] * (read(lo, rows_at(r)) - read(lo - 1, rows_at(r))) for r in range(16)]
    for l in range(lo, hi):
        v = [read(l, rows_at(r)) for r in range(16)]
        rolled = [pltpu.roll(x, 7, 0) for x in v]
        flux = [
            ky[l, rows_at(r)] * ((jnp.where(top, rolled[r + 1], rolled[r]) if r < 15 else rolled[r]) - v[r])
            for r in range(16)
        ]
        back = [pltpu.roll(x, 1, 0) for x in flux]
        ahead = []
        for r in range(16):
            rows = rows_at(r)
            fx = kx[l, rows] * (read(l + 1, rows) - v[r])
            fz = kz[l, rows] * (pltpu.roll(v[r], 127, 1) - v[r])
            down = jnp.where(bottom, back[r - 1] if r else 0.0, back[r])
            total = (aa[l, rows] * v[r] + (fx - behind[r])) + ((flux[r] - down) + (fz - pltpu.roll(fz, 1, 1)))
            finish(l, rows, v[r], total)
            ahead.append(fx)
        behind = ahead


def clear_outside(s, refs, lo, hi):
    zero = jnp.zeros((128, 128), jnp.float32)

    @pl.when(s == 0)
    def _():
        for ref in refs:
            for l in range(lo, PAD):
                ref[l] = zero

    @pl.when(s == NS - 1)
    def _():
        for ref in refs:
            for l in range(PAD + 4, hi):
                ref[l] = zero


def fine_steps(states, widths, coefficients, heat, s):
    for turn in range(4):
        a, b = states[turn % 2], states[1 - turn % 2]
        for f in range(2):
            h = widths[f] - 1 - turn

            def finish(l, rows, v, stepped):
                b[f, l, rows] = stepped + heat[l, rows]

            sweep(lambda l, rows: a[f, l, rows], finish, coefficients, PAD - h, PAD + 4 + h)
        if turn < 3:
            h = max(widths) - 1 - turn
            clear_outside(s, [b.at[0], b.at[1]], PAD - h, PAD + 4 + h)


def first_kernel(flags, pack, ev, od, out, s0, s1, cnd, heat, *coefficients):
    s = flags[1]
    core = s % 2
    for l in range(4):
        for f in range(2):
            s0[f, PAD + l] = pack[f, l]
        cnd[PAD + l] = pack[2, l]
        heat[PAD + l] = pack[3, l]

    def sides(left, right):
        for l in range(4):
            for f in range(2):
                s0[f, 1 + l] = left[f, l]
                s0[f, PAD + 4 + l] = right[f, l]
            cnd[1 + l] = left[2, l]
            cnd[PAD + 4 + l] = right[2, l]
            heat[1 + l] = left[3, l]
            heat[PAD + 4 + l] = right[3, l]

    @pl.when(core == 0)
    def _():
        sides(od, ev)

    @pl.when(core == 1)
    def _():
        sides(ev, od)

    clear_outside(s, [s0.at[0], s0.at[1], cnd], 1, EXT - 1)
    set_coefficients(cnd, *coefficients, 1, EXT - 2)
    fine_steps((s0, s1), (4, 4), coefficients, heat, s)
    for f in range(2):
        for l in range(4):
            out[f, l] = s0[f, PAD + l]


def second_kernel(
    flags, a, pack, ev, od, evc, odc, ev5, chip, e_out, w_out, tiles, s0, s1, cnd, heat, *rest
):
    coefficients, wide = rest[:4], rest[4]
    t, s = flags[0], flags[1]
    core = s % 2
    od_at = lambda i: od[128 * i : 128 * i + 128]
    for l in range(4):
        for f in range(2):
            s0[f, PAD + l] = a[f, l]
        cnd[PAD + l] = pack[2, l]
        heat[PAD + l] = pack[3, l]
    for l in range(8):
        tiles[8 + l] = chip[l]

    def sides(even, odd, even5, odd5):
        for l in range(4):
            for f in range(2):
                s0[f, even + l] = ev[f, l]
                s0[f, odd + l] = od_at(4 * f + l)
            cnd[even + l] = evc[2, l]
            cnd[odd + l] = odc[2, l]
            heat[even + l] = evc[3, l]
            heat[odd + l] = odc[3, l]
        s0[0, even5] = ev5[0:128]
        s0[0, odd5] = od_at(8)
        cnd[even5] = ev5[128:256]
        cnd[odd5] = od_at(9)

    def side_tiles(even, odd):
        for l in range(8):
            tiles[even + l] = ev5[256 + 24 * l : 280 + 24 * l]
            tiles[odd + l] = od[1280 + 24 * l : 1304 + 24 * l]

    @pl.when(core == 0)
    def _():
        sides(PAD + 4, 1, EXT - 1, 0)
        side_tiles(16, 0)

    @pl.when(core == 1)
    def _():
        sides(1, PAD + 4, 0, EXT - 1)
        side_tiles(0, 16)

    clear_outside(s, [s0.at[0], s0.at[1], cnd], 0, EXT)
    set_coefficients(cnd, *coefficients, 0, EXT - 1)
    ratio = COARSE / FINE
    for f, h in ((0, 1), (1, 0)):

        def keep(l, rows, v, stepped):
            wide[f, l, rows] = v + ratio * (stepped - v)

        sweep(lambda l, rows: s0[f, l, rows], keep, coefficients, PAD - h, PAD + 4 + h)
    fine_steps((s0, s1), (5, 4), coefficients, heat, s)
    for l in range(PAD - 1, PAD + 5):
        wide[0, l] = s0[0, l] - wide[0, l]
    clear_outside(s, [wide.at[0]], PAD - 1, PAD + 5)

    @pl.when(t != NT - 1)
    def _():
        def finish(l, rows, v, stepped):
            to = PLACE[rows.start // 8]
            e_out[to, l - PAD] = v + ratio * (stepped - v) + (s0[1, l, rows] - wide[1, l, rows])

        sweep(lambda l, rows: wide[0, l, rows], finish, coefficients, PAD, PAD + 4)
        for l in range(4):
            w_out[l] = wide[0, PAD + l]

    @pl.when(t == NT - 1)
    def _():
        for l in range(4):
            for r in range(16):
                e_out[PLACE[r], l] = s0[0, PAD + l, rows_at(r)]
            w_out[l] = a[0, l]


def region(flags, cond, halo):
    chip, place = flags[1] // 2, flags[2]
    count = 8 + 2 * halo
    shape = (count, 24, 128)
    layer = lax.broadcasted_iota(jnp.int32, shape, 0) + (chip * 8 - halo)
    row = lax.broadcasted_iota(jnp.int32, shape, 1) + (place * 8 - 8)
    col = lax.broadcasted_iota(jnp.int32, shape, 2)
    inside = (layer >= 0) & (layer < 64) & (row >= 0) & (row < 128)
    mask = inside.astype(jnp.float32)
    c = cond[8 - halo : 16 + halo] * mask
    half = 0.5 * COARSE
    kx = half * (c[:-1] + c[1:])
    ky = half * (c + pltpu.roll(c, 23, 1))
    kz = jnp.where(col < 127, half * (c + pltpu.roll(c, 127, 2)), 0.0)
    bb = jnp.where((col == 0) | (col == 127), half * c, 0.0)
    return mask, kx, ky, kz, bb


def coarse_step(v, coefficients, halo, now):
    mask, kx, ky, kz, bb = coefficients
    skip = halo - now
    count = 8 + 2 * now
    inner = slice(skip + 1, skip + count - 1)
    fx = kx[skip : skip + count - 1] * (v[1:] - v[:-1])
    mid = v[1:-1]
    fy = ky[inner] * (pltpu.roll(mid, 23, 1) - mid)
    fz = kz[inner] * (pltpu.roll(mid, 127, 2) - mid)
    change = (fx[1:] - fx[:-1]) + (fy - pltpu.roll(fy, 1, 1)) + (fz - pltpu.roll(fz, 1, 2)) - bb[inner] * mid
    return mask[inner] * (mid + change)


HALOS = (6, 4, 2)
STARTS = (0, 6, 10, 12)


def y_pieces():
    wanted = []
    for i, h in enumerate(HALOS):
        for l in range(8 + 2 * h):
            rows = h - max(h - l, l - h - 7, 0)
            if rows:
                wanted.append((rows, i, l))
    room, pieces = [], []
    for rows, i, l in sorted(wanted, reverse=True):
        tile = next((k for k, free in enumerate(room) if free >= rows), len(room))
        if tile == len(room):
            room.append(8)
        pieces.append((i, l, rows, tile, 8 - room[tile]))
        room[tile] -= rows
    return pieces, len(room)


PIECES, Y_TILES = y_pieces()


def half(core, value):
    return jnp.where(core == 0, value[0:4], value[4:8])


def slot(j):
    return (j - 1) % NT


def chips_kernel(flags, own, other, chip, send):
    def run(first, last, side):
        for j in range(NT):
            chip[j, 0:4] = first[slot(j)]
            chip[j, 4:8] = last[slot(j)]
        for q in range(4):
            for i, h in enumerate(HALOS):
                a, b = STARTS[i], STARTS[i] + h
                send[q, a:b] = chip[4 * q + i, side(h)]

    @pl.when(flags[1] % 2 == 0)
    def _():
        run(own, other, lambda h: slice(0, h))

    @pl.when(flags[1] % 2 == 1)
    def _():
        run(other, own, lambda h: slice(8 - h, 8))


def rows_kernel(flags, chip, got, swap, send):
    def run(left, right, upward):
        for q in range(4):
            for i, l, rows, tile, first in PIECES:
                h, a = HALOS[i], STARTS[i]
                pick = slice(8 - rows, 8) if upward else slice(0, rows)
                if l < h:
                    value = left[q, a + l, pick]
                elif l < h + 8:
                    value = chip[4 * q + i, l - h, pick]
                else:
                    value = right[q, a + l - h - 8, pick]
                send[q, tile, first : first + rows] = value

    @pl.when(flags[1] % 2 == 0)
    def _():
        run(got, swap, False)

    @pl.when(flags[1] % 2 == 1)
    def _():
        run(swap, got, True)


def quads_kernel(groups, flags, cond, chip, xg, xs, yg, ys, *refs):
    outs, (b0, b1, b2), coef = refs[:-8], refs[-8:-5], refs[-5:]
    core = flags[1] % 2
    for value, ref in zip(region(flags, cond, 6), coef):
        ref[...] = value
    for h, buf in zip(HALOS, (b0, b1, b2)):
        buf[...] = jnp.zeros((8 + 2 * h, 24, 128), jnp.float32)
    c = tuple(r[...] for r in coef)
    zero = jnp.zeros((4, 8, 128), jnp.float32)
    for q in groups:

        def fill(left, right, below, above):
            for i, (h, buf) in enumerate(zip(HALOS, (b0, b1, b2))):
                a = STARTS[i]
                buf[h : h + 8, 8:16] = chip[4 * q + i]
                buf[0:h, 8:16] = left[q, a : a + h]
                buf[h + 8 :, 8:16] = right[q, a : a + h]
            for i, l, rows, tile, first in PIECES:
                buf = (b0, b1, b2)[i]
                buf[l, 8 - rows : 8] = below[q, tile, first : first + rows]
                buf[l, 16 : 16 + rows] = above[q, tile, first : first + rows]

        @pl.when(core == 0)
        def _():
            fill(xg, xs, yg, ys)

        @pl.when(core == 1)
        def _():
            fill(xs, xg, ys, yg)

        p = b0[...] * c[0]
        values, partial = [chip[4 * q]], [zero]
        for i in range(3):
            h = HALOS[i]
            one = coarse_step(p, c, 6, h)
            two = coarse_step(one, c, 6, h - 1)
            partial.append(half(core, one[h - 1 : h + 7, 8:16]))
            if i < 2:
                p = two + (b1, b2)[i][...] * c[0][2 * i + 2 : 18 - 2 * i]
                values.append(p[h - 2 : h + 6, 8:16])
            else:
                values.append(two[:, 8:16] + chip[4 * q + 3])
        if q == 0:
            last, done = outs
            last[...] = values[3]
            for i in range(4):
                done[i, 0] = partial[i]
                done[i, 1] = half(core, values[i])
        else:
            p_out, zp_out, ends = outs
            ends[q - 1] = values[3]
            for i in range(4):
                p_out[4 * q - 4 + i] = half(core, values[i])
                zp_out[4 * q - 4 + i] = partial[i]


def chain_kernel(q, flags, cond, c_in, p, zp, ends, xg, xs, yg, ys, last, done, buf, *coef):
    core = flags[1] % 2
    for value, ref in zip(region(flags, cond, 8), coef):
        ref[...] = value
    buf[8:16, 8:16] = c_in[...]

    def put(left, right, below, above):
        buf[0:8, 8:16] = left[...]
        buf[16:24, 8:16] = right[...]
        buf[:, 0:8] = below[...]
        buf[:, 16:24] = above[...]

    @pl.when(core == 0)
    def _():
        put(xg, xs, yg, ys)

    @pl.when(core == 1)
    def _():
        put(xs, xg, ys, yg)

    c = tuple(r[...] for r in coef)
    v = buf[...] * c[0]
    for turn in range(8):
        v = coarse_step(v, c, 8, 8 - turn)
        tile = v[7 - turn : 15 - turn, 8:16]
        i = turn // 2
        if turn % 2 == 0:
            done[i, 0] = zp[4 * q - 4 + i] + half(core, tile)
        else:
            done[i, 1] = p[4 * q - 4 + i] + half(core, tile)
    last[...] = ends[q - 1] + tile


def final_kernel(got, w, out):
    for src in range(NT):
        rows = slice(8 * place_of(src), 8 * place_of(src) + 8)
        for l in range(4):
            out[0, l, rows] = got[src, 0, l] + w[l, rows]
            out[1, l, rows] = got[src, 1, l]


def coefficient_scratch(halo):
    counts = [8 + 2 * halo] * 5
    counts[1] -= 1
    return [pltpu.VMEM((count, 24, 128), jnp.float32) for count in counts]


def call(kernel, outs, scratches, *args, smem=True, cost=None):
    specs = [SMEM] + [VMEM] * (len(args) - 1) if smem else [VMEM] * len(args)
    return pl.pallas_call(
        kernel,
        out_shape=outs,
        in_specs=specs,
        out_specs=[VMEM] * len(outs),
        scratch_shapes=scratches,
        compiler_params=params(),
        cost_estimate=cost,
    )(*args)


def body(initial, guess, cond, source):
    t = lax.axis_index("tm")
    s = lax.axis_index("space")
    core = s % 2
    place = t ^ ((t >> 1) & 1)
    flags = jnp.stack([t, s, place, core]).astype(jnp.int32)
    swap = (jnp.arange(4) == 0)[:, None, None, None] & (t == NT - 1)
    pack = jnp.where(swap, initial[None], jnp.concatenate([guess, cond[None], source[None]]))
    ev = even(pack)
    od = odd(pack)
    layers = pltpu.VMEM((EXT, 128, 128), jnp.float32)
    fine_scratch = [pltpu.VMEM((2, EXT, 128, 128), jnp.float32)] * 2 + [layers] * 6
    (a,) = call(first_kernel, [struct(2, 4, 128, 128)], fine_scratch, flags, pack, ev, od)

    start = 8 * place
    rows_of = lambda x: lax.dynamic_slice_in_dim(jnp.pad(x, ((0, 0), (8, 8), (0, 0))), start, 24, 1)
    mine, yours = rows_of(pack[2]), rows_of(ev[2])
    chip = jnp.where(core == 0, jnp.concatenate([mine, yours]), jnp.concatenate([yours, mine]))

    ev2 = even(a)
    tail = lambda x: jnp.where(core == 0, x[0], x[3])
    nearest = lambda x: jnp.where(core == 0, x[3], x[0])
    chip_rows = chip.reshape(192, 128)
    od2 = odd(jnp.concatenate([a.reshape(1024, 128), tail(ev2[0]), tail(ev[2]), chip_rows]))
    ev5 = even(jnp.concatenate([nearest(od2[:512].reshape(4, 128, 128)), nearest(od[2]), od2[1280:]]))
    e, w, tiles = call(
        second_kernel,
        [struct(NT, 4, 8, 128), struct(4, 128, 128), struct(24, 24, 128)],
        fine_scratch + [pltpu.VMEM((2, EXT, 128, 128), jnp.float32)],
        flags, a, pack, ev2, od2, ev, od, ev5, chip,
    )
    own = lax.all_to_all(e, "tm", 0, 0)
    own, w = lax.optimization_barrier((own, w))
    w_before = lax.ppermute(w, "tm", [(i, (i + 1) % NT) for i in range(NT)])
    other = even(own)
    chips, send = call(chips_kernel, [struct(NT, 8, 8, 128), struct(4, 12, 8, 128)], [], flags, own, other)
    xg = odd(send)
    xs = even(xg)
    (send,) = call(rows_kernel, [struct(4, Y_TILES, 8, 128)], [], flags, chips, xg, xs)
    send, w_before = lax.optimization_barrier((send, w_before))
    yg = yodd(send)
    ys = even(yg)
    regions = [pltpu.VMEM((8 + 2 * h, 24, 128), jnp.float32) for h in HALOS]
    quad_scratch = regions + coefficient_scratch(6)
    last, done = call(
        functools.partial(quads_kernel, (0,)),
        [struct(8, 8, 128), struct(4, 2, 4, 8, 128)],
        quad_scratch,
        flags, tiles, chips, xg, xs, yg, ys,
    )
    p, zp, ends = call(
        functools.partial(quads_kernel, (1, 2, 3)),
        [struct(12, 4, 8, 128), struct(12, 4, 8, 128), struct(3, 8, 8, 128)],
        quad_scratch,
        flags, tiles, chips, xg, xs, yg, ys,
        cost=pl.CostEstimate(flops=30_000_000, bytes_accessed=4_000_000, transcendentals=0),
    )
    parts = [done]
    for q in (1, 2, 3):
        xg = odd(last)
        if q == 1:
            xg, p, zp, ends = lax.optimization_barrier((xg, p, zp, ends))
        xs = even(xg)
        left = jnp.where(core == 0, xg, xs)
        right = jnp.where(core == 0, xs, xg)
        yg = yodd(jnp.concatenate([left, last, right]))
        ys = even(yg)
        last, done = call(
            functools.partial(chain_kernel, q),
            [struct(8, 8, 128), struct(4, 2, 4, 8, 128)],
            [pltpu.VMEM((24, 24, 128), jnp.float32)] + coefficient_scratch(8),
            flags, tiles, last, p, zp, ends, xg, xs, yg, ys,
        )
        parts.append(done)
    back = lax.all_to_all(jnp.concatenate(parts), "tm", 0, 0)
    (out,) = call(final_kernel, [struct(2, 4, 128, 128)], [], back, w_before, smem=False)
    return out


def solution(mesh):
    placed = (
        P("space", None, None),
        P("tm", "space", None, None),
        P("space", None, None),
        P("space", None, None),
    )
    return jax.shard_map(
        body, mesh=mesh, in_specs=placed, out_specs=P("tm", "space", None, None), check_vma=False
    )
```

```python
import functools

import jax
import jax.numpy as jnp
from jax import lax
from jax.experimental import pallas as pl
from jax.experimental.pallas import tpu as pltpu
from jax.sharding import PartitionSpec as P

FINE = 0.04
COARSE = 0.16
NT = 16
NS = 16
PAD = 5
EXT = 4 + 2 * PAD
EVEN = [(i, i ^ 1) for i in range(NS)]
VMEM = pl.BlockSpec(memory_space=pltpu.VMEM)


def odd_pairs():
    pairs = []
    for t in range(NT):
        for s in range(NS):
            to = s + 1 if s % 2 else s - 1
            pairs.append((t * NS + s, t * NS + to if 0 <= to < NS else (t ^ 2) * NS + s))
    return pairs


ODD = odd_pairs()


def place_of(t, half):
    t = t ^ half
    return t ^ ((t >> 1) & 1)


PLACE = [[place_of(t, half) for t in range(NT)] for half in range(2)]
AT = [[PLACE[half].index(p) for p in range(NT)] for half in range(2)]


def chain_pairs(along_x):
    pairs = []
    for t in range(NT):
        for s in range(NS):
            step = 1 if s % 2 else -1
            half, place = s // 8, PLACE[s // 8][t]
            if not along_x:
                pairs.append((t * NS + s, AT[half][(place + step) % NT] * NS + (s ^ 1)))
            elif 0 <= s + step < NS:
                pairs.append((t * NS + s, AT[(s + step) // 8][place] * NS + s + step))
            else:
                pairs.append((t * NS + s, (t ^ 2) * NS + s))
    return pairs


XODD = chain_pairs(True)
YODD = chain_pairs(False)


def even(x):
    return lax.ppermute(x, "space", EVEN)


def odd(x):
    return lax.ppermute(x, ("tm", "space"), ODD)


def xodd(x):
    return lax.ppermute(x, ("tm", "space"), XODD)


def yodd(x):
    return lax.ppermute(x, ("tm", "space"), YODD)


def struct(*shape):
    return jax.ShapeDtypeStruct(shape, jnp.float32)


def params(mib=48):
    return pltpu.CompilerParams(vmem_limit_bytes=mib * 1024 * 1024)


def set_coefficients(cond, kx, ky, kz, aa, lo, hi):
    row = lax.broadcasted_iota(jnp.int32, (128, 128), 0)
    col = lax.broadcasted_iota(jnp.int32, (128, 128), 1)
    ghosts = (
        (row == 0).astype(jnp.float32)
        + (row == 127).astype(jnp.float32)
        + (col == 0).astype(jnp.float32)
        + (col == 127).astype(jnp.float32)
    ) * (0.5 * FINE)
    rows = (row < 127).astype(jnp.float32) * (0.5 * FINE)
    cols = (col < 127).astype(jnp.float32) * (0.5 * FINE)
    for l in range(lo, hi):
        here = cond[l]
        kx[l] = (0.5 * FINE) * (here + cond[l + 1])
        ky[l] = rows * (here + pltpu.roll(here, 127, 0))
        kz[l] = cols * (here + pltpu.roll(here, 127, 1))
        aa[l] = 1.0 - ghosts * here


def rows_at(r):
    return slice(8 * r, 8 * r + 8)


def sweep(read, finish, coefficients, lo, hi):
    kx, ky, kz, aa = coefficients
    sub = lax.broadcasted_iota(jnp.int32, (8, 128), 0)
    bottom, top = sub == 0, sub == 7
    behind = [kx[lo - 1, rows_at(r)] * (read(lo, rows_at(r)) - read(lo - 1, rows_at(r))) for r in range(16)]
    for l in range(lo, hi):
        v = [read(l, rows_at(r)) for r in range(16)]
        rolled = [pltpu.roll(x, 7, 0) for x in v]
        flux = [
            ky[l, rows_at(r)] * ((jnp.where(top, rolled[r + 1], rolled[r]) if r < 15 else rolled[r]) - v[r])
            for r in range(16)
        ]
        back = [pltpu.roll(x, 1, 0) for x in flux]
        ahead = []
        for r in range(16):
            rows = rows_at(r)
            fx = kx[l, rows] * (read(l + 1, rows) - v[r])
            fz = kz[l, rows] * (pltpu.roll(v[r], 127, 1) - v[r])
            down = jnp.where(bottom, back[r - 1] if r else 0.0, back[r])
            total = (aa[l, rows] * v[r] + (fx - behind[r])) + ((flux[r] - down) + (fz - pltpu.roll(fz, 1, 1)))
            finish(l, rows, v[r], total)
            ahead.append(fx)
        behind = ahead


def clear_outside(s, refs, lo, hi):
    zero = jnp.zeros((128, 128), jnp.float32)

    @pl.when(s == 0)
    def _():
        for ref in refs:
            for l in range(lo, PAD):
                ref[l] = zero

    @pl.when(s == NS - 1)
    def _():
        for ref in refs:
            for l in range(PAD + 4, hi):
                ref[l] = zero


def fine_steps(states, widths, coefficients, heat, s):
    for turn in range(4):
        a, b = states[turn % 2], states[1 - turn % 2]
        for f in range(2):
            h = widths[f] - 1 - turn

            def finish(l, rows, v, stepped):
                b[f, l, rows] = stepped + heat[l, rows]

            sweep(lambda l, rows: a[f, l, rows], finish, coefficients, PAD - h, PAD + 4 + h)
        if turn < 3:
            h = max(widths) - 1 - turn
            clear_outside(s, [b.at[0], b.at[1]], PAD - h, PAD + 4 + h)


def first_kernel(pack, ev, od, out, s0, s1, cnd, heat, *coefficients):
    s = lax.axis_index("space")
    core = s % 2
    for l in range(4):
        for f in range(2):
            s0[f, PAD + l] = pack[f, l]
        cnd[PAD + l] = pack[2, l]
        heat[PAD + l] = pack[3, l]

    def sides(left, right):
        for l in range(4):
            for f in range(2):
                s0[f, 1 + l] = left[f, l]
                s0[f, PAD + 4 + l] = right[f, l]
            cnd[1 + l] = left[2, l]
            cnd[PAD + 4 + l] = right[2, l]
            heat[1 + l] = left[3, l]
            heat[PAD + 4 + l] = right[3, l]

    @pl.when(core == 0)
    def _():
        sides(od, ev)

    @pl.when(core == 1)
    def _():
        sides(ev, od)

    clear_outside(s, [s0.at[0], s0.at[1], cnd], 1, EXT - 1)
    set_coefficients(cnd, *coefficients, 1, EXT - 2)
    fine_steps((s0, s1), (4, 4), coefficients, heat, s)
    for f in range(2):
        for l in range(4):
            out[f, l] = s0[f, PAD + l]


def second_kernel(
    a, pack, ev, od, evc, odc, ev5, e_out, w_out, s0, s1, cnd, heat, *rest
):
    coefficients, wide = rest[:4], rest[4]
    t, s = lax.axis_index("tm"), lax.axis_index("space")
    core = s % 2
    od_at = lambda i: od[128 * i : 128 * i + 128]
    for l in range(4):
        for f in range(2):
            s0[f, PAD + l] = a[f, l]
        cnd[PAD + l] = pack[2, l]
        heat[PAD + l] = pack[3, l]

    def sides(even, odd, even5, odd5):
        for l in range(4):
            for f in range(2):
                s0[f, even + l] = ev[f, l]
                s0[f, odd + l] = od_at(4 * f + l)
            cnd[even + l] = evc[2, l]
            cnd[odd + l] = odc[2, l]
            heat[even + l] = evc[3, l]
            heat[odd + l] = odc[3, l]
        s0[0, even5] = ev5[0:128]
        s0[0, odd5] = od_at(8)
        cnd[even5] = ev5[128:256]
        cnd[odd5] = od_at(9)

    @pl.when(core == 0)
    def _():
        sides(PAD + 4, 1, EXT - 1, 0)

    @pl.when(core == 1)
    def _():
        sides(1, PAD + 4, 0, EXT - 1)

    clear_outside(s, [s0.at[0], s0.at[1], cnd], 0, EXT)
    set_coefficients(cnd, *coefficients, 0, EXT - 1)
    ratio = COARSE / FINE
    for f, h in ((0, 1), (1, 0)):

        def keep(l, rows, v, stepped):
            wide[f, l, rows] = v + ratio * (stepped - v)

        sweep(lambda l, rows: s0[f, l, rows], keep, coefficients, PAD - h, PAD + 4 + h)
    fine_steps((s0, s1), (5, 4), coefficients, heat, s)
    for l in range(PAD - 1, PAD + 5):
        wide[0, l] = s0[0, l] - wide[0, l]
    clear_outside(s, [wide.at[0]], PAD - 1, PAD + 5)

    def leave(h):
        @pl.when((s // 8 == h) & (t != NT - 1))
        def _():
            def finish(l, rows, v, stepped):
                to = AT[h][rows.start // 8]
                e_out[to, l - PAD] = v + ratio * (stepped - v) + (s0[1, l, rows] - wide[1, l, rows])

            sweep(lambda l, rows: wide[0, l, rows], finish, coefficients, PAD, PAD + 4)
            for l in range(4):
                w_out[l] = wide[0, PAD + l]

        @pl.when((s // 8 == h) & (t == NT - 1))
        def _():
            for l in range(4):
                for r in range(16):
                    e_out[AT[h][r], l] = s0[0, PAD + l, rows_at(r)]
                w_out[l] = a[0, l]

    leave(0)
    leave(1)


def region(cond, halo):
    t, s = lax.axis_index("tm"), lax.axis_index("space")
    chip, place = s // 2, place_of(t, s // 8)
    count = 8 + 2 * halo
    shape = (count, 24, 128)
    layer = lax.broadcasted_iota(jnp.int32, shape, 0) + (chip * 8 - halo)
    row = lax.broadcasted_iota(jnp.int32, shape, 1) + (place * 8 - 8)
    col = lax.broadcasted_iota(jnp.int32, shape, 2)
    inside = (layer >= 0) & (layer < 64) & (row >= 0) & (row < 128)
    mask = inside.astype(jnp.float32)
    c = cond[8 - halo : 16 + halo] * mask
    half = 0.5 * COARSE
    kx = half * (c[:-1] + c[1:])
    ky = half * (c + pltpu.roll(c, 23, 1))
    kz = jnp.where(col < 127, half * (c + pltpu.roll(c, 127, 2)), 0.0)
    bb = jnp.where((col == 0) | (col == 127), half * c, 0.0)
    return mask, kx, ky, kz, bb


def coarse_step(v, coefficients, halo, now):
    mask, kx, ky, kz, bb = coefficients
    skip = halo - now
    count = 8 + 2 * now
    inner = slice(skip + 1, skip + count - 1)
    fx = kx[skip : skip + count - 1] * (v[1:] - v[:-1])
    mid = v[1:-1]
    fy = ky[inner] * (pltpu.roll(mid, 23, 1) - mid)
    fz = kz[inner] * (pltpu.roll(mid, 127, 2) - mid)
    change = (fx[1:] - fx[:-1]) + (fy - pltpu.roll(fy, 1, 1)) + (fz - pltpu.roll(fz, 1, 2)) - bb[inner] * mid
    return mask[inner] * (mid + change)


HALOS = (6, 4, 2)
STARTS = (0, 6, 10, 12)


def y_pieces():
    wanted = []
    for i, h in enumerate(HALOS):
        for l in range(8 + 2 * h):
            rows = h - max(h - l, l - h - 7, 0)
            if rows:
                wanted.append((rows, i, l))
    room, pieces = [], []
    for rows, i, l in sorted(wanted, reverse=True):
        tile = next((k for k, free in enumerate(room) if free >= rows), len(room))
        if tile == len(room):
            room.append(8)
        pieces.append((i, l, rows, tile, 8 - room[tile]))
        room[tile] -= rows
    return pieces, len(room)


PIECES, Y_TILES = y_pieces()


def half(core, value):
    return jnp.where(core == 0, value[0:4], value[4:8])


def slot(j):
    return (j - 1) % NT


def chips_kernel(own, other, cond, cond_got, cond_swap, chip, send, tiles):
    tiles[8:16] = cond[...]

    def run(first, last, side, left, right):
        tiles[0:8] = left[...]
        tiles[16:24] = right[...]
        for j in range(NT):
            chip[j, 0:4] = first[slot(j)]
            chip[j, 4:8] = last[slot(j)]
        for q in range(4):
            for i, h in enumerate(HALOS):
                a, b = STARTS[i], STARTS[i] + h
                send[q, a:b] = chip[4 * q + i, side(h)]

    @pl.when(lax.axis_index("space") % 2 == 0)
    def _():
        run(own, other, lambda h: slice(0, h), cond_got, cond_swap)

    @pl.when(lax.axis_index("space") % 2 == 1)
    def _():
        run(other, own, lambda h: slice(8 - h, 8), cond_swap, cond_got)


def rows_kernel(chip, got, swap, send):
    def run(left, right, upward):
        for q in range(4):
            for i, l, rows, tile, first in PIECES:
                h, a = HALOS[i], STARTS[i]
                pick = slice(8 - rows, 8) if upward else slice(0, rows)
                if l < h:
                    value = left[q, a + l, pick]
                elif l < h + 8:
                    value = chip[4 * q + i, l - h, pick]
                else:
                    value = right[q, a + l - h - 8, pick]
                send[q, tile, first : first + rows] = value

    @pl.when(lax.axis_index("space") % 2 == 0)
    def _():
        run(got, swap, False)

    @pl.when(lax.axis_index("space") % 2 == 1)
    def _():
        run(swap, got, True)


def quads_kernel(groups, cond, chip, xg, xs, yg, ys, *refs):
    outs, (b0, b1, b2), coef = refs[:-8], refs[-8:-5], refs[-5:]
    core = lax.axis_index("space") % 2
    for value, ref in zip(region(cond, 6), coef):
        ref[...] = value
    for h, buf in zip(HALOS, (b0, b1, b2)):
        buf[...] = jnp.zeros((8 + 2 * h, 24, 128), jnp.float32)
    c = tuple(r[...] for r in coef)
    zero = jnp.zeros((4, 8, 128), jnp.float32)
    for q in groups:

        def fill(left, right, below, above):
            for i, (h, buf) in enumerate(zip(HALOS, (b0, b1, b2))):
                a = STARTS[i]
                buf[h : h + 8, 8:16] = chip[4 * q + i]
                buf[0:h, 8:16] = left[q, a : a + h]
                buf[h + 8 :, 8:16] = right[q, a : a + h]
            for i, l, rows, tile, first in PIECES:
                buf = (b0, b1, b2)[i]
                buf[l, 8 - rows : 8] = below[q, tile, first : first + rows]
                buf[l, 16 : 16 + rows] = above[q, tile, first : first + rows]

        @pl.when(core == 0)
        def _():
            fill(xg, xs, yg, ys)

        @pl.when(core == 1)
        def _():
            fill(xs, xg, ys, yg)

        p = b0[...] * c[0]
        values, partial = [chip[4 * q]], [zero]
        for i in range(3):
            h = HALOS[i]
            one = coarse_step(p, c, 6, h)
            two = coarse_step(one, c, 6, h - 1)
            partial.append(half(core, one[h - 1 : h + 7, 8:16]))
            if i < 2:
                p = two + (b1, b2)[i][...] * c[0][2 * i + 2 : 18 - 2 * i]
                values.append(p[h - 2 : h + 6, 8:16])
            else:
                values.append(two[:, 8:16] + chip[4 * q + 3])
        if q == 0:
            last, done = outs
            last[...] = values[3]
            for i in range(4):
                done[i, 0] = partial[i]
                done[i, 1] = half(core, values[i])
        else:
            p_out, zp_out, ends = outs
            ends[q - 1] = values[3]
            for i in range(4):
                p_out[4 * q - 4 + i] = half(core, values[i])
                zp_out[4 * q - 4 + i] = partial[i]


def chain_kernel(q, cond, c_in, p, zp, ends, xg, xs, yg, ys, last, done, buf, *coef):
    core = lax.axis_index("space") % 2
    for value, ref in zip(region(cond, 8), coef):
        ref[...] = value
    buf[8:16, 8:16] = c_in[...]

    def put(left, right, below, above):
        buf[0:8, 8:16] = left[...]
        buf[16:24, 8:16] = right[...]
        buf[:, 0:8] = below[...]
        buf[:, 16:24] = above[...]

    @pl.when(core == 0)
    def _():
        put(xg, xs, yg, ys)

    @pl.when(core == 1)
    def _():
        put(xs, xg, ys, yg)

    c = tuple(r[...] for r in coef)
    v = buf[...] * c[0]
    for turn in range(8):
        v = coarse_step(v, c, 8, 8 - turn)
        tile = v[7 - turn : 15 - turn, 8:16]
        i = turn // 2
        if turn % 2 == 0:
            done[i, 0] = zp[4 * q - 4 + i] + half(core, tile)
        else:
            done[i, 1] = p[4 * q - 4 + i] + half(core, tile)
    last[...] = ends[q - 1] + tile


def final_kernel(got, w, out):
    def run(h):
        for src in range(NT):
            rows = rows_at(PLACE[h][src])
            for l in range(4):
                out[0, l, rows] = got[src, 0, l] + w[l, rows]
                out[1, l, rows] = got[src, 1, l]

    @pl.when(lax.axis_index("space") < 8)
    def _():
        run(0)

    @pl.when(lax.axis_index("space") >= 8)
    def _():
        run(1)


def coefficient_scratch(halo):
    counts = [8 + 2 * halo] * 5
    counts[1] -= 1
    return [pltpu.VMEM((count, 24, 128), jnp.float32) for count in counts]


def call(kernel, outs, scratches, *args, cost=None):
    return pl.pallas_call(
        kernel,
        out_shape=outs,
        in_specs=[VMEM] * len(args),
        out_specs=[VMEM] * len(outs),
        scratch_shapes=scratches,
        compiler_params=params(),
        cost_estimate=cost,
    )(*args)


def body(initial, guess, cond, source):
    t = lax.axis_index("tm")
    s = lax.axis_index("space")
    core = s % 2
    place = place_of(t, s // 8)
    swap = (jnp.arange(4) == 0)[:, None, None, None] & (t == NT - 1)
    pack = jnp.where(swap, initial[None], jnp.concatenate([guess, cond[None], source[None]]))
    ev = even(pack)
    od = odd(pack)
    start = 8 * place
    rows_of = lambda x: lax.dynamic_slice_in_dim(jnp.pad(x, ((0, 0), (8, 8), (0, 0))), start, 24, 1)
    mine, yours = rows_of(pack[2]), rows_of(ev[2])
    chip = jnp.where(core == 0, jnp.concatenate([mine, yours]), jnp.concatenate([yours, mine]))
    c_got = xodd(chip)

    layers = pltpu.VMEM((EXT, 128, 128), jnp.float32)
    fine_scratch = [pltpu.VMEM((2, EXT, 128, 128), jnp.float32)] * 2 + [layers] * 6
    (a,) = call(first_kernel, [struct(2, 4, 128, 128)], fine_scratch, pack, ev, od)

    a, c_got = lax.optimization_barrier((a, c_got))
    ev2 = even(a)
    tail = lambda x: jnp.where(core == 0, x[0], x[3])
    nearest = lambda x: jnp.where(core == 0, x[3], x[0])
    od2 = odd(jnp.concatenate([a.reshape(1024, 128), tail(ev2[0]), tail(ev[2])]))
    ev5 = even(jnp.concatenate([nearest(od2[:512].reshape(4, 128, 128)), nearest(od[2])]))
    ev5, c_got = lax.optimization_barrier((ev5, c_got))
    c_swap = even(c_got)
    e, w = call(
        second_kernel,
        [struct(NT, 4, 8, 128), struct(4, 128, 128)],
        fine_scratch + [pltpu.VMEM((2, EXT, 128, 128), jnp.float32)],
        a, pack, ev2, od2, ev, od, ev5,
    )
    e, w, c_swap = lax.optimization_barrier((e, w, c_swap))
    own = lax.all_to_all(e, "tm", 0, 0)
    own, w = lax.optimization_barrier((own, w))
    w_before = lax.ppermute(w, "tm", [(i, (i + 1) % NT) for i in range(NT)])
    other = even(own)
    chips, send, tiles = call(
        chips_kernel,
        [struct(NT, 8, 8, 128), struct(4, 12, 8, 128), struct(24, 24, 128)],
        [],
        own, other, chip, c_got, c_swap,
    )
    xg = xodd(send)
    xs = even(xg)
    (send,) = call(rows_kernel, [struct(4, Y_TILES, 8, 128)], [], chips, xg, xs)
    send, w_before = lax.optimization_barrier((send, w_before))
    yg = yodd(send)
    ys = even(yg)
    regions = [pltpu.VMEM((8 + 2 * h, 24, 128), jnp.float32) for h in HALOS]
    quad_scratch = regions + coefficient_scratch(6)
    last, done = call(
        functools.partial(quads_kernel, (0,)),
        [struct(8, 8, 128), struct(4, 2, 4, 8, 128)],
        quad_scratch,
        tiles, chips, xg, xs, yg, ys,
    )
    p, zp, ends = call(
        functools.partial(quads_kernel, (1, 2, 3)),
        [struct(12, 4, 8, 128), struct(12, 4, 8, 128), struct(3, 8, 8, 128)],
        quad_scratch,
        tiles, chips, xg, xs, yg, ys,
        cost=pl.CostEstimate(flops=30_000_000, bytes_accessed=4_000_000, transcendentals=0),
    )
    parts = [done]
    for q in (1, 2, 3):
        xg = xodd(last)
        if q == 1:
            xg, p, zp, ends = lax.optimization_barrier((xg, p, zp, ends))
        xs = even(xg)
        left = jnp.where(core == 0, xg, xs)
        right = jnp.where(core == 0, xs, xg)
        yg = yodd(jnp.concatenate([left, last, right]))
        ys = even(yg)
        last, done = call(
            functools.partial(chain_kernel, q),
            [struct(8, 8, 128), struct(4, 2, 4, 8, 128)],
            [pltpu.VMEM((24, 24, 128), jnp.float32)] + coefficient_scratch(8),
            tiles, last, p, zp, ends, xg, xs, yg, ys,
        )
        parts.append(done)
    back = lax.all_to_all(jnp.concatenate(parts), "tm", 0, 0)
    (out,) = call(final_kernel, [struct(2, 4, 128, 128)], [], back, w_before)
    return out


def solution(mesh):
    placed = (
        P("space", None, None),
        P("tm", "space", None, None),
        P("space", None, None),
        P("space", None, None),
    )
    return jax.shard_map(
        body, mesh=mesh, in_specs=placed, out_specs=P("tm", "space", None, None), check_vma=False
    )
```

```python
import functools

import jax
import jax.numpy as jnp
from jax import lax
from jax.experimental import pallas as pl
from jax.experimental.pallas import tpu as pltpu
from jax.sharding import PartitionSpec as P

FINE = 0.04
COARSE = 0.16
NT = 16
NS = 16
PAD = 5
EXT = 4 + 2 * PAD
EVEN = [(i, i ^ 1) for i in range(NS)]
VMEM = pl.BlockSpec(memory_space=pltpu.VMEM)


def odd_pairs():
    pairs = []
    for t in range(NT):
        for s in range(NS):
            to = s + 1 if s % 2 else s - 1
            pairs.append((t * NS + s, t * NS + to if 0 <= to < NS else (t ^ 2) * NS + s))
    return pairs


ODD = odd_pairs()


def place_of(t, half):
    t = t ^ half
    return t ^ ((t >> 1) & 1)


PLACE = [[place_of(t, half) for t in range(NT)] for half in range(2)]
AT = [[PLACE[half].index(p) for p in range(NT)] for half in range(2)]


def chain_pairs(along_x):
    pairs = []
    for t in range(NT):
        for s in range(NS):
            step = 1 if s % 2 else -1
            half, place = s // 8, PLACE[s // 8][t]
            if not along_x:
                pairs.append((t * NS + s, AT[half][(place + step) % NT] * NS + (s ^ 1)))
            elif 0 <= s + step < NS:
                pairs.append((t * NS + s, AT[(s + step) // 8][place] * NS + s + step))
            else:
                pairs.append((t * NS + s, (t ^ 2) * NS + s))
    return pairs


XODD = chain_pairs(True)
YODD = chain_pairs(False)


def even(x):
    return lax.ppermute(x, "space", EVEN)


def odd(x):
    return lax.ppermute(x, ("tm", "space"), ODD)


def xodd(x):
    return lax.ppermute(x, ("tm", "space"), XODD)


def yodd(x):
    return lax.ppermute(x, ("tm", "space"), YODD)


def struct(*shape):
    return jax.ShapeDtypeStruct(shape, jnp.float32)


def params(mib=48):
    return pltpu.CompilerParams(vmem_limit_bytes=mib * 1024 * 1024)


def set_coefficients(cond, kx, ky, kz, aa, lo, hi):
    row = lax.broadcasted_iota(jnp.int32, (128, 128), 0)
    col = lax.broadcasted_iota(jnp.int32, (128, 128), 1)
    ghosts = (
        (row == 0).astype(jnp.float32)
        + (row == 127).astype(jnp.float32)
        + (col == 0).astype(jnp.float32)
        + (col == 127).astype(jnp.float32)
    ) * (0.5 * FINE)
    rows = (row < 127).astype(jnp.float32) * (0.5 * FINE)
    cols = (col < 127).astype(jnp.float32) * (0.5 * FINE)
    for l in range(lo, hi):
        here = cond[l]
        kx[l] = (0.5 * FINE) * (here + cond[l + 1])
        ky[l] = rows * (here + pltpu.roll(here, 127, 0))
        kz[l] = cols * (here + pltpu.roll(here, 127, 1))
        aa[l] = 1.0 - ghosts * here


def rows_at(r):
    return slice(8 * r, 8 * r + 8)


def sweep(read, finish, coefficients, lo, hi):
    kx, ky, kz, aa = coefficients
    sub = lax.broadcasted_iota(jnp.int32, (8, 128), 0)
    bottom, top = sub == 0, sub == 7
    behind = [kx[lo - 1, rows_at(r)] * (read(lo, rows_at(r)) - read(lo - 1, rows_at(r))) for r in range(16)]
    for l in range(lo, hi):
        v = [read(l, rows_at(r)) for r in range(16)]
        rolled = [pltpu.roll(x, 7, 0) for x in v]
        flux = [
            ky[l, rows_at(r)] * ((jnp.where(top, rolled[r + 1], rolled[r]) if r < 15 else rolled[r]) - v[r])
            for r in range(16)
        ]
        back = [pltpu.roll(x, 1, 0) for x in flux]
        ahead = []
        for r in range(16):
            rows = rows_at(r)
            fx = kx[l, rows] * (read(l + 1, rows) - v[r])
            fz = kz[l, rows] * (pltpu.roll(v[r], 127, 1) - v[r])
            down = jnp.where(bottom, back[r - 1] if r else 0.0, back[r])
            total = (aa[l, rows] * v[r] + (fx - behind[r])) + ((flux[r] - down) + (fz - pltpu.roll(fz, 1, 1)))
            finish(l, rows, v[r], total)
            ahead.append(fx)
        behind = ahead


def clear_outside(s, refs, lo, hi):
    zero = jnp.zeros((128, 128), jnp.float32)

    @pl.when(s == 0)
    def _():
        for ref in refs:
            for l in range(lo, PAD):
                ref[l] = zero

    @pl.when(s == NS - 1)
    def _():
        for ref in refs:
            for l in range(PAD + 4, hi):
                ref[l] = zero


def fine_steps(states, widths, coefficients, heat, s):
    for turn in range(4):
        a, b = states[turn % 2], states[1 - turn % 2]
        for f in range(2):
            h = widths[f] - 1 - turn

            def finish(l, rows, v, stepped):
                b[f, l, rows] = stepped + heat[l, rows]

            sweep(lambda l, rows: a[f, l, rows], finish, coefficients, PAD - h, PAD + 4 + h)
        if turn < 3:
            h = max(widths) - 1 - turn
            clear_outside(s, [b.at[0], b.at[1]], PAD - h, PAD + 4 + h)


def first_kernel(pack, ev, od, out, s0, s1, cnd, heat, *coefficients):
    s = lax.axis_index("space")
    core = s % 2
    for l in range(4):
        for f in range(2):
            s0[f, PAD + l] = pack[f, l]
        cnd[PAD + l] = pack[2, l]
        heat[PAD + l] = pack[3, l]

    def sides(left, right):
        for l in range(4):
            for f in range(2):
                s0[f, 1 + l] = left[f, l]
                s0[f, PAD + 4 + l] = right[f, l]
            cnd[1 + l] = left[2, l]
            cnd[PAD + 4 + l] = right[2, l]
            heat[1 + l] = left[3, l]
            heat[PAD + 4 + l] = right[3, l]

    @pl.when(core == 0)
    def _():
        sides(od, ev)

    @pl.when(core == 1)
    def _():
        sides(ev, od)

    clear_outside(s, [s0.at[0], s0.at[1], cnd], 1, EXT - 1)
    set_coefficients(cnd, *coefficients, 1, EXT - 2)
    fine_steps((s0, s1), (4, 4), coefficients, heat, s)
    for f in range(2):
        for l in range(4):
            out[f, l] = s0[f, PAD + l]


def second_kernel(
    a, pack, ev, od, evc, odc, low, high, e_out, w_out, s0, s1, cnd, heat, *rest
):
    coefficients, wide = rest[:4], rest[4]
    t, s = lax.axis_index("tm"), lax.axis_index("space")
    core = s % 2
    for l in range(4):
        for f in range(2):
            s0[f, PAD + l] = a[f, l]
        cnd[PAD + l] = pack[2, l]
        heat[PAD + l] = pack[3, l]

    def sides(even, odd):
        for l in range(4):
            for f in range(2):
                s0[f, even + l] = ev[f, l]
                s0[f, odd + l] = od[f, l]
            cnd[even + l] = evc[2, l]
            cnd[odd + l] = odc[2, l]
            heat[even + l] = evc[3, l]
            heat[odd + l] = odc[3, l]

    @pl.when(core == 0)
    def _():
        sides(PAD + 4, 1)

    @pl.when(core == 1)
    def _():
        sides(1, PAD + 4)

    clear_outside(s, [s0.at[0], s0.at[1], cnd], 1, EXT - 1)
    zero = jnp.zeros((128, 128), jnp.float32)
    inside = s > 1
    s0[0, 0] = jnp.where(inside, low[0], zero)
    cnd[0] = jnp.where(inside, low[1], zero)
    inside = s < NS - 2
    s0[0, EXT - 1] = jnp.where(inside, high[0], zero)
    cnd[EXT - 1] = jnp.where(inside, high[1], zero)
    set_coefficients(cnd, *coefficients, 0, EXT - 1)
    ratio = COARSE / FINE
    for f, h in ((0, 1), (1, 0)):

        def keep(l, rows, v, stepped):
            wide[f, l, rows] = v + ratio * (stepped - v)

        sweep(lambda l, rows: s0[f, l, rows], keep, coefficients, PAD - h, PAD + 4 + h)
    fine_steps((s0, s1), (5, 4), coefficients, heat, s)
    for l in range(PAD - 1, PAD + 5):
        wide[0, l] = s0[0, l] - wide[0, l]
    clear_outside(s, [wide.at[0]], PAD - 1, PAD + 5)

    def leave(h):
        @pl.when((s // 8 == h) & (t != NT - 1))
        def _():
            def finish(l, rows, v, stepped):
                to = AT[h][rows.start // 8]
                e_out[to, l - PAD] = v + ratio * (stepped - v) + (s0[1, l, rows] - wide[1, l, rows])

            sweep(lambda l, rows: wide[0, l, rows], finish, coefficients, PAD, PAD + 4)
            for l in range(4):
                w_out[l] = wide[0, PAD + l]

        @pl.when((s // 8 == h) & (t == NT - 1))
        def _():
            for l in range(4):
                for r in range(16):
                    e_out[AT[h][r], l] = s0[0, PAD + l, rows_at(r)]
                w_out[l] = a[0, l]

    leave(0)
    leave(1)


def region(cond, halo):
    t, s = lax.axis_index("tm"), lax.axis_index("space")
    chip, place = s // 2, place_of(t, s // 8)
    count = 8 + 2 * halo
    shape = (count, 24, 128)
    layer = lax.broadcasted_iota(jnp.int32, shape, 0) + (chip * 8 - halo)
    row = lax.broadcasted_iota(jnp.int32, shape, 1) + (place * 8 - 8)
    col = lax.broadcasted_iota(jnp.int32, shape, 2)
    inside = (layer >= 0) & (layer < 64) & (row >= 0) & (row < 128)
    mask = inside.astype(jnp.float32)
    c = cond[8 - halo : 16 + halo] * mask
    half = 0.5 * COARSE
    kx = half * (c[:-1] + c[1:])
    ky = half * (c + pltpu.roll(c, 23, 1))
    kz = jnp.where(col < 127, half * (c + pltpu.roll(c, 127, 2)), 0.0)
    bb = jnp.where((col == 0) | (col == 127), half * c, 0.0)
    return mask, kx, ky, kz, bb


def coarse_step(v, coefficients, halo, now):
    mask, kx, ky, kz, bb = coefficients
    skip = halo - now
    count = 8 + 2 * now
    inner = slice(skip + 1, skip + count - 1)
    fx = kx[skip : skip + count - 1] * (v[1:] - v[:-1])
    mid = v[1:-1]
    fy = ky[inner] * (pltpu.roll(mid, 23, 1) - mid)
    fz = kz[inner] * (pltpu.roll(mid, 127, 2) - mid)
    change = (fx[1:] - fx[:-1]) + (fy - pltpu.roll(fy, 1, 1)) + (fz - pltpu.roll(fz, 1, 2)) - bb[inner] * mid
    return mask[inner] * (mid + change)


HALOS = (6, 4, 2)
STARTS = (0, 6, 10, 12)


def y_pieces():
    wanted = []
    for i, h in enumerate(HALOS):
        for l in range(8 + 2 * h):
            rows = h - max(h - l, l - h - 7, 0)
            if rows:
                wanted.append((rows, i, l))
    room, pieces = [], []
    for rows, i, l in sorted(wanted, reverse=True):
        tile = next((k for k, free in enumerate(room) if free >= rows), len(room))
        if tile == len(room):
            room.append(8)
        pieces.append((i, l, rows, tile, 8 - room[tile]))
        room[tile] -= rows
    return pieces, len(room)


PIECES, Y_TILES = y_pieces()


def half(core, value):
    return jnp.where(core == 0, value[0:4], value[4:8])


def slot(j):
    return (j - 1) % NT


def chips_kernel(own, other, cond, cond_got, cond_swap, chip, send, tiles):
    tiles[8:16] = cond[...]

    def run(first, last, side, left, right):
        tiles[0:8] = left[...]
        tiles[16:24] = right[...]
        for j in range(NT):
            chip[j, 0:4] = first[slot(j)]
            chip[j, 4:8] = last[slot(j)]
        for q in range(4):
            for i, h in enumerate(HALOS):
                a, b = STARTS[i], STARTS[i] + h
                send[q, a:b] = chip[4 * q + i, side(h)]

    @pl.when(lax.axis_index("space") % 2 == 0)
    def _():
        run(own, other, lambda h: slice(0, h), cond_got, cond_swap)

    @pl.when(lax.axis_index("space") % 2 == 1)
    def _():
        run(other, own, lambda h: slice(8 - h, 8), cond_swap, cond_got)


def rows_kernel(chip, got, swap, send):
    def run(left, right, upward):
        for q in range(4):
            for i, l, rows, tile, first in PIECES:
                h, a = HALOS[i], STARTS[i]
                pick = slice(8 - rows, 8) if upward else slice(0, rows)
                if l < h:
                    value = left[q, a + l, pick]
                elif l < h + 8:
                    value = chip[4 * q + i, l - h, pick]
                else:
                    value = right[q, a + l - h - 8, pick]
                send[q, tile, first : first + rows] = value

    @pl.when(lax.axis_index("space") % 2 == 0)
    def _():
        run(got, swap, False)

    @pl.when(lax.axis_index("space") % 2 == 1)
    def _():
        run(swap, got, True)


def quads_kernel(groups, cond, chip, xg, xs, yg, ys, *refs):
    outs, (b0, b1, b2), coef = refs[:-8], refs[-8:-5], refs[-5:]
    core = lax.axis_index("space") % 2
    for value, ref in zip(region(cond, 6), coef):
        ref[...] = value
    for h, buf in zip(HALOS, (b0, b1, b2)):
        buf[...] = jnp.zeros((8 + 2 * h, 24, 128), jnp.float32)
    c = tuple(r[...] for r in coef)
    zero = jnp.zeros((4, 8, 128), jnp.float32)
    for q in groups:

        def fill(left, right, below, above):
            for i, (h, buf) in enumerate(zip(HALOS, (b0, b1, b2))):
                a = STARTS[i]
                buf[h : h + 8, 8:16] = chip[4 * q + i]
                buf[0:h, 8:16] = left[q, a : a + h]
                buf[h + 8 :, 8:16] = right[q, a : a + h]
            for i, l, rows, tile, first in PIECES:
                buf = (b0, b1, b2)[i]
                buf[l, 8 - rows : 8] = below[q, tile, first : first + rows]
                buf[l, 16 : 16 + rows] = above[q, tile, first : first + rows]

        @pl.when(core == 0)
        def _():
            fill(xg, xs, yg, ys)

        @pl.when(core == 1)
        def _():
            fill(xs, xg, ys, yg)

        p = b0[...] * c[0]
        values, partial = [chip[4 * q]], [zero]
        for i in range(3):
            h = HALOS[i]
            one = coarse_step(p, c, 6, h)
            two = coarse_step(one, c, 6, h - 1)
            partial.append(half(core, one[h - 1 : h + 7, 8:16]))
            if i < 2:
                p = two + (b1, b2)[i][...] * c[0][2 * i + 2 : 18 - 2 * i]
                values.append(p[h - 2 : h + 6, 8:16])
            else:
                values.append(two[:, 8:16] + chip[4 * q + 3])
        if q == 0:
            last, done = outs
            last[...] = values[3]
            for i in range(4):
                done[i, 0] = partial[i]
                done[i, 1] = half(core, values[i])
        else:
            p_out, zp_out, ends = outs
            ends[q - 1] = values[3]
            for i in range(4):
                p_out[4 * q - 4 + i] = half(core, values[i])
                zp_out[4 * q - 4 + i] = partial[i]


def chain_kernel(q, cond, c_in, p, zp, ends, xg, xs, yg, ys, last, done, buf, *coef):
    core = lax.axis_index("space") % 2
    for value, ref in zip(region(cond, 8), coef):
        ref[...] = value
    buf[8:16, 8:16] = c_in[...]

    def put(left, right, below, above):
        buf[0:8, 8:16] = left[...]
        buf[16:24, 8:16] = right[...]
        buf[:, 0:8] = below[...]
        buf[:, 16:24] = above[...]

    @pl.when(core == 0)
    def _():
        put(xg, xs, yg, ys)

    @pl.when(core == 1)
    def _():
        put(xs, xg, ys, yg)

    c = tuple(r[...] for r in coef)
    v = buf[...] * c[0]
    for turn in range(8):
        v = coarse_step(v, c, 8, 8 - turn)
        tile = v[7 - turn : 15 - turn, 8:16]
        i = turn // 2
        if turn % 2 == 0:
            done[i, 0] = zp[4 * q - 4 + i] + half(core, tile)
        else:
            done[i, 1] = p[4 * q - 4 + i] + half(core, tile)
    last[...] = ends[q - 1] + tile


def final_kernel(got, w, out):
    def run(h):
        for src in range(NT):
            rows = rows_at(PLACE[h][src])
            for l in range(4):
                out[0, l, rows] = got[src, 0, l] + w[l, rows]
                out[1, l, rows] = got[src, 1, l]

    @pl.when(lax.axis_index("space") < 8)
    def _():
        run(0)

    @pl.when(lax.axis_index("space") >= 8)
    def _():
        run(1)


def coefficient_scratch(halo):
    counts = [8 + 2 * halo] * 5
    counts[1] -= 1
    return [pltpu.VMEM((count, 24, 128), jnp.float32) for count in counts]


def call(kernel, outs, scratches, *args, cost=None):
    return pl.pallas_call(
        kernel,
        out_shape=outs,
        in_specs=[VMEM] * len(args),
        out_specs=[VMEM] * len(outs),
        scratch_shapes=scratches,
        compiler_params=params(),
        cost_estimate=cost,
    )(*args)


def body(initial, guess, cond, source):
    t = lax.axis_index("tm")
    s = lax.axis_index("space")
    core = s % 2
    place = place_of(t, s // 8)
    swap = (jnp.arange(4) == 0)[:, None, None, None] & (t == NT - 1)
    pack = jnp.where(swap, initial[None], jnp.concatenate([guess, cond[None], source[None]]))
    ev = even(pack)
    od = odd(pack)
    start = 8 * place
    rows_of = lambda x: lax.dynamic_slice_in_dim(jnp.pad(x, ((0, 0), (8, 8), (0, 0))), start, 24, 1)
    mine, yours = rows_of(pack[2]), rows_of(ev[2])
    chip = jnp.where(core == 0, jnp.concatenate([mine, yours]), jnp.concatenate([yours, mine]))
    c_got = xodd(chip)

    layers = pltpu.VMEM((EXT, 128, 128), jnp.float32)
    fine_scratch = [pltpu.VMEM((2, EXT, 128, 128), jnp.float32)] * 2 + [layers] * 6
    (a,) = call(first_kernel, [struct(2, 4, 128, 128)], fine_scratch, pack, ev, od)

    a, c_got = lax.optimization_barrier((a, c_got))
    ev2 = even(a)
    od2 = odd(a)
    low = lax.ppermute(jnp.stack([a[0, 3], pack[2, 3]]), "space", [(i, (i + 2) % NS) for i in range(NS)])
    high = lax.ppermute(jnp.stack([a[0, 0], pack[2, 0]]), "space", [(i, (i - 2) % NS) for i in range(NS)])
    od2, c_got = lax.optimization_barrier((od2, c_got))
    c_swap = even(c_got)
    e, w = call(
        second_kernel,
        [struct(NT, 4, 8, 128), struct(4, 128, 128)],
        fine_scratch + [pltpu.VMEM((2, EXT, 128, 128), jnp.float32)],
        a, pack, ev2, od2, ev, od, low, high,
    )
    e, w, c_swap = lax.optimization_barrier((e, w, c_swap))
    own = lax.all_to_all(e, "tm", 0, 0)
    own, w = lax.optimization_barrier((own, w))
    w_before = lax.ppermute(w, "tm", [(i, (i + 1) % NT) for i in range(NT)])
    other = even(own)
    chips, send, tiles = call(
        chips_kernel,
        [struct(NT, 8, 8, 128), struct(4, 12, 8, 128), struct(24, 24, 128)],
        [],
        own, other, chip, c_got, c_swap,
    )
    xg = xodd(send)
    xs = even(xg)
    (send,) = call(rows_kernel, [struct(4, Y_TILES, 8, 128)], [], chips, xg, xs)
    send, w_before = lax.optimization_barrier((send, w_before))
    yg = yodd(send)
    ys = even(yg)
    regions = [pltpu.VMEM((8 + 2 * h, 24, 128), jnp.float32) for h in HALOS]
    quad_scratch = regions + coefficient_scratch(6)
    last, done = call(
        functools.partial(quads_kernel, (0,)),
        [struct(8, 8, 128), struct(4, 2, 4, 8, 128)],
        quad_scratch,
        tiles, chips, xg, xs, yg, ys,
    )
    p, zp, ends = call(
        functools.partial(quads_kernel, (1, 2, 3)),
        [struct(12, 4, 8, 128), struct(12, 4, 8, 128), struct(3, 8, 8, 128)],
        quad_scratch,
        tiles, chips, xg, xs, yg, ys,
        cost=pl.CostEstimate(flops=30_000_000, bytes_accessed=4_000_000, transcendentals=0),
    )
    parts = [done]
    for q in (1, 2, 3):
        xg = xodd(last)
        if q == 1:
            xg, p, zp, ends = lax.optimization_barrier((xg, p, zp, ends))
        xs = even(xg)
        left = jnp.where(core == 0, xg, xs)
        right = jnp.where(core == 0, xs, xg)
        yg = yodd(jnp.concatenate([left, last, right]))
        ys = even(yg)
        last, done = call(
            functools.partial(chain_kernel, q),
            [struct(8, 8, 128), struct(4, 2, 4, 8, 128)],
            [pltpu.VMEM((24, 24, 128), jnp.float32)] + coefficient_scratch(8),
            tiles, last, p, zp, ends, xg, xs, yg, ys,
        )
        parts.append(done)
    back = lax.all_to_all(jnp.concatenate(parts), "tm", 0, 0)
    (out,) = call(final_kernel, [struct(2, 4, 128, 128)], [], back, w_before)
    return out


def solution(mesh):
    placed = (
        P("space", None, None),
        P("tm", "space", None, None),
        P("space", None, None),
        P("space", None, None),
    )
    return jax.shard_map(
        body, mesh=mesh, in_specs=placed, out_specs=P("tm", "space", None, None), check_vma=False
    )
```

```python
import functools

import jax
import jax.numpy as jnp
from jax import lax
from jax.experimental import pallas as pl
from jax.experimental.pallas import tpu as pltpu
from jax.sharding import PartitionSpec as P

FINE = 0.04
COARSE = 0.16
NT = 16
NS = 16
PAD = 5
EXT = 4 + 2 * PAD
EVEN = [(i, i ^ 1) for i in range(NS)]
VMEM = pl.BlockSpec(memory_space=pltpu.VMEM)


def odd_pairs():
    pairs = []
    for t in range(NT):
        for s in range(NS):
            to = s + 1 if s % 2 else s - 1
            pairs.append((t * NS + s, t * NS + to if 0 <= to < NS else (t ^ 2) * NS + s))
    return pairs


ODD = odd_pairs()


def place_of(t, half):
    t = t ^ half
    return t ^ ((t >> 1) & 1)


PLACE = [[place_of(t, half) for t in range(NT)] for half in range(2)]
AT = [[PLACE[half].index(p) for p in range(NT)] for half in range(2)]


def chain_pairs(along_x):
    pairs = []
    for t in range(NT):
        for s in range(NS):
            step = 1 if s % 2 else -1
            half, place = s // 8, PLACE[s // 8][t]
            if not along_x:
                pairs.append((t * NS + s, AT[half][(place + step) % NT] * NS + (s ^ 1)))
            elif 0 <= s + step < NS:
                pairs.append((t * NS + s, AT[(s + step) // 8][place] * NS + s + step))
            else:
                pairs.append((t * NS + s, (t ^ 2) * NS + s))
    return pairs


XODD = chain_pairs(True)
YODD = chain_pairs(False)


def even(x):
    return lax.ppermute(x, "space", EVEN)


def odd(x):
    return lax.ppermute(x, ("tm", "space"), ODD)


def xodd(x):
    return lax.ppermute(x, ("tm", "space"), XODD)


def yodd(x):
    return lax.ppermute(x, ("tm", "space"), YODD)


def struct(*shape):
    return jax.ShapeDtypeStruct(shape, jnp.float32)


def params(mib=48):
    return pltpu.CompilerParams(vmem_limit_bytes=mib * 1024 * 1024)


def set_coefficients(cond, kx, ky, kz, aa, lo, hi):
    row = lax.broadcasted_iota(jnp.int32, (128, 128), 0)
    col = lax.broadcasted_iota(jnp.int32, (128, 128), 1)
    ghosts = (
        (row == 0).astype(jnp.float32)
        + (row == 127).astype(jnp.float32)
        + (col == 0).astype(jnp.float32)
        + (col == 127).astype(jnp.float32)
    ) * (0.5 * FINE)
    rows = (row < 127).astype(jnp.float32) * (0.5 * FINE)
    cols = (col < 127).astype(jnp.float32) * (0.5 * FINE)
    for l in range(lo, hi):
        here = cond[l]
        kx[l] = (0.5 * FINE) * (here + cond[l + 1])
        ky[l] = rows * (here + pltpu.roll(here, 127, 0))
        kz[l] = cols * (here + pltpu.roll(here, 127, 1))
        aa[l] = 1.0 - ghosts * here


def rows_at(r):
    return slice(8 * r, 8 * r + 8)


def sweep(read, finish, coefficients, lo, hi):
    kx, ky, kz, aa = coefficients
    sub = lax.broadcasted_iota(jnp.int32, (8, 128), 0)
    bottom, top = sub == 0, sub == 7
    behind = [kx[lo - 1, rows_at(r)] * (read(lo, rows_at(r)) - read(lo - 1, rows_at(r))) for r in range(16)]
    for l in range(lo, hi):
        v = [read(l, rows_at(r)) for r in range(16)]
        rolled = [pltpu.roll(x, 7, 0) for x in v]
        flux = [
            ky[l, rows_at(r)] * ((jnp.where(top, rolled[r + 1], rolled[r]) if r < 15 else rolled[r]) - v[r])
            for r in range(16)
        ]
        back = [pltpu.roll(x, 1, 0) for x in flux]
        ahead = []
        for r in range(16):
            rows = rows_at(r)
            fx = kx[l, rows] * (read(l + 1, rows) - v[r])
            fz = kz[l, rows] * (pltpu.roll(v[r], 127, 1) - v[r])
            down = jnp.where(bottom, back[r - 1] if r else 0.0, back[r])
            total = (aa[l, rows] * v[r] + (fx - behind[r])) + ((flux[r] - down) + (fz - pltpu.roll(fz, 1, 1)))
            finish(l, rows, v[r], total)
            ahead.append(fx)
        behind = ahead


def clear_outside(s, refs, lo, hi):
    zero = jnp.zeros((128, 128), jnp.float32)

    @pl.when(s == 0)
    def _():
        for ref in refs:
            for l in range(lo, PAD):
                ref[l] = zero

    @pl.when(s == NS - 1)
    def _():
        for ref in refs:
            for l in range(PAD + 4, hi):
                ref[l] = zero


def fine_steps(states, widths, coefficients, heat, s):
    for turn in range(4):
        a, b = states[turn % 2], states[1 - turn % 2]
        for f in range(2):
            h = widths[f] - 1 - turn

            def finish(l, rows, v, stepped):
                b[f, l, rows] = stepped + heat[l, rows]

            sweep(lambda l, rows: a[f, l, rows], finish, coefficients, PAD - h, PAD + 4 + h)
        if turn < 3:
            h = max(widths) - 1 - turn
            clear_outside(s, [b.at[0], b.at[1]], PAD - h, PAD + 4 + h)


def first_kernel(pack, ev, od, out, s0, s1, cnd, heat, *coefficients):
    s = lax.axis_index("space")
    core = s % 2
    for l in range(4):
        for f in range(2):
            s0[f, PAD + l] = pack[f, l]
        cnd[PAD + l] = pack[2, l]
        heat[PAD + l] = pack[3, l]

    def sides(left, right):
        for l in range(4):
            for f in range(2):
                s0[f, 1 + l] = left[f, l]
                s0[f, PAD + 4 + l] = right[f, l]
            cnd[1 + l] = left[2, l]
            cnd[PAD + 4 + l] = right[2, l]
            heat[1 + l] = left[3, l]
            heat[PAD + 4 + l] = right[3, l]

    @pl.when(core == 0)
    def _():
        sides(od, ev)

    @pl.when(core == 1)
    def _():
        sides(ev, od)

    clear_outside(s, [s0.at[0], s0.at[1], cnd], 1, EXT - 1)
    set_coefficients(cnd, *coefficients, 1, EXT - 2)
    fine_steps((s0, s1), (4, 4), coefficients, heat, s)
    for f in range(2):
        for l in range(4):
            out[f, l] = s0[f, PAD + l]


def second_kernel(
    a, pack, ev, od, evc, odc, low, high, e_out, w_out, s0, s1, cnd, heat, *rest
):
    coefficients, wide = rest[:4], rest[4]
    t, s = lax.axis_index("tm"), lax.axis_index("space")
    core = s % 2
    for l in range(4):
        for f in range(2):
            s0[f, PAD + l] = a[f, l]
        cnd[PAD + l] = pack[2, l]
        heat[PAD + l] = pack[3, l]

    def sides(even, odd):
        for l in range(4):
            for f in range(2):
                s0[f, even + l] = ev[f, l]
                s0[f, odd + l] = od[f, l]
            cnd[even + l] = evc[2, l]
            cnd[odd + l] = odc[2, l]
            heat[even + l] = evc[3, l]
            heat[odd + l] = odc[3, l]

    @pl.when(core == 0)
    def _():
        sides(PAD + 4, 1)

    @pl.when(core == 1)
    def _():
        sides(1, PAD + 4)

    clear_outside(s, [s0.at[0], s0.at[1], cnd], 1, EXT - 1)
    zero = jnp.zeros((128, 128), jnp.float32)
    inside = s > 1
    s0[0, 0] = jnp.where(inside, low[0], zero)
    cnd[0] = jnp.where(inside, low[1], zero)
    inside = s < NS - 2
    s0[0, EXT - 1] = jnp.where(inside, high[0], zero)
    cnd[EXT - 1] = jnp.where(inside, high[1], zero)
    set_coefficients(cnd, *coefficients, 0, EXT - 1)
    ratio = COARSE / FINE
    for f, h in ((0, 1), (1, 0)):

        def keep(l, rows, v, stepped):
            wide[f, l, rows] = v + ratio * (stepped - v)

        sweep(lambda l, rows: s0[f, l, rows], keep, coefficients, PAD - h, PAD + 4 + h)
    fine_steps((s0, s1), (5, 4), coefficients, heat, s)
    for l in range(PAD - 1, PAD + 5):
        wide[0, l] = s0[0, l] - wide[0, l]
    clear_outside(s, [wide.at[0]], PAD - 1, PAD + 5)

    def leave(h):
        @pl.when((s // 8 == h) & (t != NT - 1))
        def _():
            def finish(l, rows, v, stepped):
                to = AT[h][rows.start // 8]
                e_out[to, l - PAD] = v + ratio * (stepped - v) + (s0[1, l, rows] - wide[1, l, rows])

            sweep(lambda l, rows: wide[0, l, rows], finish, coefficients, PAD, PAD + 4)
            for l in range(4):
                w_out[l] = wide[0, PAD + l]

        @pl.when((s // 8 == h) & (t == NT - 1))
        def _():
            for l in range(4):
                for r in range(16):
                    e_out[AT[h][r], l] = s0[0, PAD + l, rows_at(r)]
                w_out[l] = a[0, l]

    leave(0)
    leave(1)


def region(cond, halo):
    t, s = lax.axis_index("tm"), lax.axis_index("space")
    chip, place = s // 2, place_of(t, s // 8)
    count = 8 + 2 * halo
    shape = (count, 24, 128)
    layer = lax.broadcasted_iota(jnp.int32, shape, 0) + (chip * 8 - halo)
    row = lax.broadcasted_iota(jnp.int32, shape, 1) + (place * 8 - 8)
    col = lax.broadcasted_iota(jnp.int32, shape, 2)
    inside = (layer >= 0) & (layer < 64) & (row >= 0) & (row < 128)
    mask = inside.astype(jnp.float32)
    c = cond[8 - halo : 16 + halo] * mask
    half = 0.5 * COARSE
    kx = half * (c[:-1] + c[1:])
    ky = half * (c + pltpu.roll(c, 23, 1))
    kz = jnp.where(col < 127, half * (c + pltpu.roll(c, 127, 2)), 0.0)
    bb = jnp.where((col == 0) | (col == 127), half * c, 0.0)
    return mask, kx, ky, kz, bb


def coarse_step(v, coefficients, halo, now):
    mask, kx, ky, kz, bb = coefficients
    skip = halo - now
    count = 8 + 2 * now
    inner = slice(skip + 1, skip + count - 1)
    fx = kx[skip : skip + count - 1] * (v[1:] - v[:-1])
    mid = v[1:-1]
    fy = ky[inner] * (pltpu.roll(mid, 23, 1) - mid)
    fz = kz[inner] * (pltpu.roll(mid, 127, 2) - mid)
    change = (fx[1:] - fx[:-1]) + (fy - pltpu.roll(fy, 1, 1)) + (fz - pltpu.roll(fz, 1, 2)) - bb[inner] * mid
    return mask[inner] * (mid + change)


HALOS = (6, 4, 2)
STARTS = (0, 6, 10, 12)


def y_pieces():
    wanted = []
    for i, h in enumerate(HALOS):
        for l in range(8 + 2 * h):
            rows = h - max(h - l, l - h - 7, 0)
            if rows:
                wanted.append((rows, i, l))
    room, pieces = [], []
    for rows, i, l in sorted(wanted, reverse=True):
        tile = next((k for k, free in enumerate(room) if free >= rows), len(room))
        if tile == len(room):
            room.append(8)
        pieces.append((i, l, rows, tile, 8 - room[tile]))
        room[tile] -= rows
    return pieces, len(room)


PIECES, Y_TILES = y_pieces()


def half(core, value):
    return jnp.where(core == 0, value[0:4], value[4:8])


def slot(j):
    return (j - 1) % NT


def chips_kernel(own, other, cond, cond_got, cond_swap, chip, send, tiles):
    tiles[8:16] = cond[...]

    def run(first, last, side, left, right):
        tiles[0:8] = left[...]
        tiles[16:24] = right[...]
        for j in range(NT):
            chip[j, 0:4] = first[slot(j)]
            chip[j, 4:8] = last[slot(j)]
        for q in range(4):
            for i, h in enumerate(HALOS):
                a, b = STARTS[i], STARTS[i] + h
                send[q, a:b] = chip[4 * q + i, side(h)]

    @pl.when(lax.axis_index("space") % 2 == 0)
    def _():
        run(own, other, lambda h: slice(0, h), cond_got, cond_swap)

    @pl.when(lax.axis_index("space") % 2 == 1)
    def _():
        run(other, own, lambda h: slice(8 - h, 8), cond_swap, cond_got)


def rows_kernel(chip, got, swap, send):
    def run(left, right, upward):
        for q in range(4):
            for i, l, rows, tile, first in PIECES:
                h, a = HALOS[i], STARTS[i]
                pick = slice(8 - rows, 8) if upward else slice(0, rows)
                if l < h:
                    value = left[q, a + l, pick]
                elif l < h + 8:
                    value = chip[4 * q + i, l - h, pick]
                else:
                    value = right[q, a + l - h - 8, pick]
                send[q, tile, first : first + rows] = value

    @pl.when(lax.axis_index("space") % 2 == 0)
    def _():
        run(got, swap, False)

    @pl.when(lax.axis_index("space") % 2 == 1)
    def _():
        run(swap, got, True)


def quads_kernel(groups, cond, chip, xg, xs, yg, ys, *refs):
    outs, (b0, b1, b2), coef = refs[:-8], refs[-8:-5], refs[-5:]
    core = lax.axis_index("space") % 2
    for value, ref in zip(region(cond, 6), coef):
        ref[...] = value
    if 0 not in groups:
        for value, ref in zip(region(cond, 8), outs[3:]):
            ref[...] = value
    for h, buf in zip(HALOS, (b0, b1, b2)):
        buf[...] = jnp.zeros((8 + 2 * h, 24, 128), jnp.float32)
    c = tuple(r[...] for r in coef)
    zero = jnp.zeros((4, 8, 128), jnp.float32)
    for q in groups:

        def fill(left, right, below, above):
            for i, (h, buf) in enumerate(zip(HALOS, (b0, b1, b2))):
                a = STARTS[i]
                buf[h : h + 8, 8:16] = chip[4 * q + i]
                buf[0:h, 8:16] = left[q, a : a + h]
                buf[h + 8 :, 8:16] = right[q, a : a + h]
            for i, l, rows, tile, first in PIECES:
                buf = (b0, b1, b2)[i]
                buf[l, 8 - rows : 8] = below[q, tile, first : first + rows]
                buf[l, 16 : 16 + rows] = above[q, tile, first : first + rows]

        @pl.when(core == 0)
        def _():
            fill(xg, xs, yg, ys)

        @pl.when(core == 1)
        def _():
            fill(xs, xg, ys, yg)

        p = b0[...] * c[0]
        values, partial = [chip[4 * q]], [zero]
        for i in range(3):
            h = HALOS[i]
            one = coarse_step(p, c, 6, h)
            two = coarse_step(one, c, 6, h - 1)
            partial.append(half(core, one[h - 1 : h + 7, 8:16]))
            if i < 2:
                p = two + (b1, b2)[i][...] * c[0][2 * i + 2 : 18 - 2 * i]
                values.append(p[h - 2 : h + 6, 8:16])
            else:
                values.append(two[:, 8:16] + chip[4 * q + 3])
        if q == 0:
            last, done = outs
            last[...] = values[3]
            for i in range(4):
                done[i, 0] = partial[i]
                done[i, 1] = half(core, values[i])
        else:
            p_out, zp_out, ends = outs[:3]
            ends[q - 1] = values[3]
            for i in range(4):
                p_out[4 * q - 4 + i] = half(core, values[i])
                zp_out[4 * q - 4 + i] = partial[i]


def chain_kernel(q, c_in, p, zp, ends, xg, xs, yg, ys, mask, kx, ky, kz, bb, done, *rest):
    buf = rest[-1]
    core = lax.axis_index("space") % 2
    buf[8:16, 8:16] = c_in[...]

    def put(left, right, below, above):
        buf[0:8, 8:16] = left[...]
        buf[16:24, 8:16] = right[...]
        buf[:, 0:8] = below[...]
        buf[:, 16:24] = above[...]

    @pl.when(core == 0)
    def _():
        put(xg, xs, yg, ys)

    @pl.when(core == 1)
    def _():
        put(xs, xg, ys, yg)

    c = tuple(r[...] for r in (mask, kx, ky, kz, bb))
    v = buf[...] * c[0]
    for turn in range(8):
        v = coarse_step(v, c, 8, 8 - turn)
        tile = v[7 - turn : 15 - turn, 8:16]
        i = turn // 2
        if turn % 2 == 0:
            done[i, 0] = zp[4 * q - 4 + i] + half(core, tile)
        else:
            done[i, 1] = p[4 * q - 4 + i] + half(core, tile)
    if q < 3:
        rest[0][...] = ends[q - 1] + tile


def final_kernel(got, w, out):
    def run(h):
        for src in range(NT):
            rows = rows_at(PLACE[h][src])
            for l in range(4):
                out[0, l, rows] = got[src, 0, l] + w[l, rows]
                out[1, l, rows] = got[src, 1, l]

    @pl.when(lax.axis_index("space") < 8)
    def _():
        run(0)

    @pl.when(lax.axis_index("space") >= 8)
    def _():
        run(1)


def coefficient_scratch(halo):
    counts = [8 + 2 * halo] * 5
    counts[1] -= 1
    return [pltpu.VMEM((count, 24, 128), jnp.float32) for count in counts]


def call(kernel, outs, scratches, *args, cost=None):
    return pl.pallas_call(
        kernel,
        out_shape=outs,
        in_specs=[VMEM] * len(args),
        out_specs=[VMEM] * len(outs),
        scratch_shapes=scratches,
        compiler_params=params(),
        cost_estimate=cost,
    )(*args)


def body(initial, guess, cond, source):
    t = lax.axis_index("tm")
    s = lax.axis_index("space")
    core = s % 2
    place = place_of(t, s // 8)
    swap = (jnp.arange(4) == 0)[:, None, None, None] & (t == NT - 1)
    pack = jnp.where(swap, initial[None], jnp.concatenate([guess, cond[None], source[None]]))
    ev = even(pack)
    od = odd(pack)
    start = 8 * place
    rows_of = lambda x: lax.dynamic_slice_in_dim(jnp.pad(x, ((0, 0), (8, 8), (0, 0))), start, 24, 1)
    mine, yours = rows_of(pack[2]), rows_of(ev[2])
    chip = jnp.where(core == 0, jnp.concatenate([mine, yours]), jnp.concatenate([yours, mine]))
    c_got = xodd(chip)

    layers = pltpu.VMEM((EXT, 128, 128), jnp.float32)
    fine_scratch = [pltpu.VMEM((2, EXT, 128, 128), jnp.float32)] * 2 + [layers] * 6
    (a,) = call(first_kernel, [struct(2, 4, 128, 128)], fine_scratch, pack, ev, od)

    a, c_got = lax.optimization_barrier((a, c_got))
    ev2 = even(a)
    od2 = odd(a)
    low = lax.ppermute(jnp.stack([a[0, 3], pack[2, 3]]), "space", [(i, (i + 2) % NS) for i in range(NS)])
    high = lax.ppermute(jnp.stack([a[0, 0], pack[2, 0]]), "space", [(i, (i - 2) % NS) for i in range(NS)])
    od2, c_got = lax.optimization_barrier((od2, c_got))
    c_swap = even(c_got)
    e, w = call(
        second_kernel,
        [struct(NT, 4, 8, 128), struct(4, 128, 128)],
        fine_scratch + [pltpu.VMEM((2, EXT, 128, 128), jnp.float32)],
        a, pack, ev2, od2, ev, od, low, high,
    )
    e, w, c_swap = lax.optimization_barrier((e, w, c_swap))
    own = lax.all_to_all(e, "tm", 0, 0)
    own, w = lax.optimization_barrier((own, w))
    w_before = lax.ppermute(w, "tm", [(i, (i + 1) % NT) for i in range(NT)])
    other = even(own)
    chips, send, tiles = call(
        chips_kernel,
        [struct(NT, 8, 8, 128), struct(4, 12, 8, 128), struct(24, 24, 128)],
        [],
        own, other, chip, c_got, c_swap,
    )
    xg = xodd(send)
    xs = even(xg)
    (send,) = call(rows_kernel, [struct(4, Y_TILES, 8, 128)], [], chips, xg, xs)
    send, w_before = lax.optimization_barrier((send, w_before))
    yg = yodd(send)
    ys = even(yg)
    regions = [pltpu.VMEM((8 + 2 * h, 24, 128), jnp.float32) for h in HALOS]
    quad_scratch = regions + coefficient_scratch(6)
    last, done = call(
        functools.partial(quads_kernel, (0,)),
        [struct(8, 8, 128), struct(4, 2, 4, 8, 128)],
        quad_scratch,
        tiles, chips, xg, xs, yg, ys,
    )
    p, zp, ends, *chain_coefficients = call(
        functools.partial(quads_kernel, (1, 2, 3)),
        [struct(12, 4, 8, 128), struct(12, 4, 8, 128), struct(3, 8, 8, 128)]
        + [struct(24 - (k == 1), 24, 128) for k in range(5)],
        quad_scratch,
        tiles, chips, xg, xs, yg, ys,
        cost=pl.CostEstimate(flops=30_000_000, bytes_accessed=4_000_000, transcendentals=0),
    )
    parts = [done]
    for q in (1, 2, 3):
        xg = xodd(last)
        if q == 1:
            xg, p, zp, ends = lax.optimization_barrier((xg, p, zp, ends))
        xs = even(xg)
        left = jnp.where(core == 0, xg, xs)
        right = jnp.where(core == 0, xs, xg)
        yg = yodd(jnp.concatenate([left, last, right]))
        ys = even(yg)
        done, *last = call(
            functools.partial(chain_kernel, q),
            [struct(4, 2, 4, 8, 128)] + [struct(8, 8, 128)] * (q < 3),
            [pltpu.VMEM((24, 24, 128), jnp.float32)],
            last, p, zp, ends, xg, xs, yg, ys, *chain_coefficients,
        )
        parts.append(done)
        last = last[0] if last else None
    back = lax.all_to_all(jnp.concatenate(parts), "tm", 0, 0)
    (out,) = call(final_kernel, [struct(2, 4, 128, 128)], [], back, w_before)
    return out


def solution(mesh):
    placed = (
        P("space", None, None),
        P("tm", "space", None, None),
        P("space", None, None),
        P("space", None, None),
    )
    return jax.shard_map(
        body, mesh=mesh, in_specs=placed, out_specs=P("tm", "space", None, None), check_vma=False
    )
```
